32 devices in a mesh: gx: 4 (over x, core), gy: 8 (over z, y).
Axes of the slice: x: 2, y: 2, z: 4, core: 2. Of those that a mesh axis runs over, the one named last changes fastest.
Arguments:
- fields: bfloat16 [672, 672, 1536], P('gx', 'gy'), may hold values from -16 to 16
- x_factor: bfloat16 [672, 336], replicated, may hold values from -0.00030517578 to 0.00030517578
- running_r: float32 [672, 672], replicated, as said below
Outputs:
- new_r: float32 [672, 672], P('gy', 'gx')
The draws below stay inside these ranges and needn't reach their ends.
Inputs may be any that keep to these rules, and one draw needn't show every extreme that they name: `running_r`: upper triangular with a positive diagonal.
All inputs are finite; a program needn't handle non-finite values.
Results may differ from the reference program's by a relative error of at most 0.0003.
Values may be sent and summed in bfloat16 or wider, within the bound.
No kernel may reach another device: no remote copies, remote signals or barrier semaphores. Data moves between devices by JAX's collectives and lax.ppermute only.
A program may use at most 256 MiB of HBM per device.

```python
import jax
import jax.numpy as jnp
from jax import lax

NX = 672
NY = 672
NR = 336
CELLS = 1536


def draw_running_r(key, part):
    first, second = jax.random.split(jax.random.fold_in(key, 7))
    upper = jax.random.normal(first, (NY, NY), jnp.float32) * NY ** (-0.5)
    diag_vals = jnp.exp(jax.random.uniform(second, (NY,), jnp.float32, jnp.log(0.5), jnp.log(2.0)))
    return jnp.triu(upper, 1) + jnp.diag(diag_vals)


def draw_fields(key, part):
    first = jax.random.fold_in(jax.random.fold_in(key, 11), 0)
    values = jnp.clip(jax.random.normal(first, (NX, NY, CELLS), jnp.float32), -6.0, 6.0)
    return values.astype(jnp.bfloat16)


def bell_draw(stream_key, dims, spread, reach, held_as=jnp.bfloat16):
    values = jax.random.normal(stream_key, dims, jnp.float32) * spread
    return jnp.minimum(jnp.maximum(values, -reach), reach).astype(held_as)


def setup_inputs(seed: int = 0) -> dict:
    arg_keys = jax.random.split(jax.random.key(seed), 4)
    fields = draw_fields(jax.random.fold_in(arg_keys[3], 71), 0)
    x_factor = bell_draw(arg_keys[1], (NX, NR), (NX * NR * CELLS) ** -0.5, 0.00030517578)
    running_r = draw_running_r(jax.random.fold_in(arg_keys[3], 71), 0)
    return {"fields": fields, "x_factor": x_factor, "running_r": running_r}


def reference(fields, x_factor, running_r):

    def one_block(gram_sum, index):
        block = lax.dynamic_slice_in_dim(fields, (index * 128).astype(jnp.int32), 128, 2)
        projected = lax.dot_general(x_factor.astype(jnp.float32), block.reshape(NX, NY * 128).astype(jnp.float32), (((0,), (0,)), ((), ())), preferred_element_type=jnp.float32).astype(jnp.bfloat16)
        wide = projected.reshape(NR, NY, 128).astype(jnp.float32)
        return (gram_sum + jnp.einsum('ayc,azc->yz', wide, wide, precision=lax.Precision.HIGHEST), None)
    start_gram = jnp.zeros((NY, NY), jnp.float32)
    gram_sum, _ = lax.scan(one_block, start_gram, jnp.arange(CELLS // 128, dtype=jnp.int32))
    total = jnp.dot(running_r.T.astype(jnp.float32), running_r.astype(jnp.float32), precision=lax.Precision.HIGHEST, preferred_element_type=jnp.float32) + gram_sum
    return jnp.linalg.cholesky(total).T
```

```python
import functools

import jax
import jax.numpy as jnp
from jax import lax
from jax.experimental import pallas as pl
from jax.experimental.pallas import tpu as pltpu
from jax.sharding import PartitionSpec as P

LANES = 128
PITCH = 96
VMEM_BYTES = 56 * 1024 * 1024


def y_pieces(rows):
    leftover = rows % 16
    main = rows - leftover
    pieces = []
    start = 0
    while start < main:
        size = min(32, main - start)
        pieces.append([start, size, 0])
        start += size
    pieces[-1][2] = leftover
    return [tuple(p) for p in pieces]


def project_kernel(start, main, left, rank, share, scalars, fields, got, factor, outs, own, wide, sem):
    rows = main + left
    column = pl.multiple_of(scalars[0], LANES)
    copy = pltpu.make_async_copy(
        fields.at[pl.ds(start, rows), :, pl.ds(column, LANES)], own, sem
    )
    copy.start()
    copy.wait()
    blocks = [own] + list(got)

    def one_pair(pair, _):
        y = pair * 2
        total = None
        for index, block in enumerate(blocks):
            right = jnp.concatenate([block[y], block[y + 1]], axis=1)
            term = jnp.dot(factor[index], right, preferred_element_type=jnp.float32)
            total = term if total is None else total + term
        at = pl.multiple_of(y * rank, 8)
        wide[pl.ds(at, rank), :] = total[:, :LANES]
        wide[pl.ds(at + rank, rank), :] = total[:, LANES:]
        return 0

    lax.fori_loop(0, rows // 2, one_pair, 0)

    for part, out in enumerate(outs):
        first = scalars[1 + part]

        def one_row(i, _):
            picked = wide[pl.ds(first + i, main, stride=rank), :]
            out[pl.ds(pl.multiple_of(i * main, 16), main), :] = picked.astype(jnp.bfloat16)
            return 0

        lax.fori_loop(0, share, one_row, 0)
        if left:
            per = 16 // left
            for group in range(0, share, per):
                count = min(per, share - group)
                tile = [
                    wide[pl.ds(main * rank + first + group + k, left, stride=rank), :]
                    for k in range(count)
                ]
                tile = jnp.concatenate(tile, axis=0).astype(jnp.bfloat16)
                at = share * main + group * left
                out[at : at + count * left, :] = tile


def project(fields, got, factor, scalars, piece, share):
    start, main, left = piece
    rows = main + left
    rank = factor.shape[1]
    depth = fields.shape[1]
    parts = scalars.shape[0] - 1
    n_got = len(got)

    def body(scalars, fields, *rest):
        got = rest[:n_got]
        factor = rest[n_got]
        outs = rest[n_got + 1 : n_got + 1 + parts]
        own, wide, sem = rest[n_got + 1 + parts :]
        project_kernel(
            start, main, left, rank, share, scalars, fields, got, factor, outs, own, wide, sem
        )

    vmem = pl.BlockSpec(memory_space=pltpu.VMEM)
    out_rows = share * rows
    return pl.pallas_call(
        body,
        out_shape=[jax.ShapeDtypeStruct((out_rows, LANES), jnp.bfloat16)] * parts,
        in_specs=[pl.BlockSpec(memory_space=pltpu.SMEM), pl.BlockSpec(memory_space=pl.ANY)]
        + [vmem] * (n_got + 1),
        out_specs=[vmem] * parts,
        scratch_shapes=[
            pltpu.VMEM((rows, depth, LANES), jnp.bfloat16),
            pltpu.VMEM((rows * rank, LANES), jnp.float32),
            pltpu.SemaphoreType.DMA,
        ],
        compiler_params=pltpu.CompilerParams(vmem_limit_bytes=VMEM_BYTES),
        cost_estimate=pl.CostEstimate(
            flops=2 * rows * LANES * rank * depth * (n_got + 1),
            bytes_accessed=2 * rows * LANES * (depth * (n_got + 1) + rank),
            transcendentals=0,
        ),
        name="project",
    )(scalars, fields, *got, factor)


def gram_kernel(pieces, share, sources, blocks, carried, out, fibres):
    n_pieces = len(pieces)
    parts = len(blocks) // n_pieces
    whole = fibres.shape[0]

    for part in range(parts):
        base = pl.multiple_of(sources[part] * PITCH, 16)

        def one_row(i, _):
            at = pl.multiple_of(i * LANES, LANES)
            for index, (start, main, _left) in enumerate(pieces):
                block = blocks[part * n_pieces + index]
                fibres[pl.ds(base + start, main), pl.ds(at, LANES)] = block[
                    pl.ds(pl.multiple_of(i * main, 16), main), :
                ]
            return 0

        lax.fori_loop(0, share, one_row, 0)
        for index, (start, main, left) in enumerate(pieces):
            if not left:
                continue
            block = blocks[part * n_pieces + index]
            per = 16 // left
            for group in range(0, share, per):
                count = min(per, share - group)
                at = share * main + group * left
                tile = block[at : at + count * left, :].astype(jnp.float32)
                for k in range(count):
                    rows = tile[k * left : (k + 1) * left, :]
                    rows = jnp.concatenate(
                        [rows, jnp.zeros((16 - left, LANES), jnp.float32)], axis=0
                    )
                    fibres[
                        pl.ds(base + start + main, 16), (group + k) * LANES : (group + k + 1) * LANES
                    ] = rows.astype(jnp.bfloat16)

    step = 256
    for i in range(0, whole, step):
        for j in range(0, whole, step):
            if j < i:
                out[i : i + step, j : j + step] = jnp.zeros((step, step), jnp.float32)
                continue
            product = lax.dot_general(
                fibres[i : i + step, :],
                fibres[j : j + step, :],
                (((1,), (1,)), ((), ())),
                preferred_element_type=jnp.float32,
            )
            if carried is not None:
                product = product + carried[i : i + step, j : j + step]
            out[i : i + step, j : j + step] = product


def gram(blocks, carried, sources, pieces, share):
    parts = sources.shape[0]
    whole = parts * PITCH
    n_blocks = len(blocks)

    def body(sources, *rest):
        blocks = rest[:n_blocks]
        if carried is None:
            out, fibres = rest[n_blocks:]
            before = None
        else:
            before, out, fibres = rest[n_blocks:]
        gram_kernel(pieces, share, sources, blocks, before, out, fibres)

    vmem = pl.BlockSpec(memory_space=pltpu.VMEM)
    extra = [] if carried is None else [carried]
    return pl.pallas_call(
        body,
        out_shape=jax.ShapeDtypeStruct((whole, whole), jnp.float32),
        in_specs=[pl.BlockSpec(memory_space=pltpu.SMEM)] + [vmem] * (n_blocks + len(extra)),
        out_specs=vmem,
        scratch_shapes=[pltpu.VMEM((whole, share * LANES), jnp.bfloat16)],
        compiler_params=pltpu.CompilerParams(vmem_limit_bytes=VMEM_BYTES),
        cost_estimate=pl.CostEstimate(
            flops=2 * whole * whole * share * LANES,
            bytes_accessed=2 * whole * share * LANES + 8 * whole * whole,
            transcendentals=0,
        ),
        name="gram",
    )(sources, *blocks, *extra)


def slice_out(upper_r):
    row_block = upper_r.shape[0] // lax.axis_size("gy")
    col_block = upper_r.shape[1] // lax.axis_size("gx")
    return lax.dynamic_slice(
        upper_r,
        (lax.axis_index("gy") * row_block, lax.axis_index("gx") * col_block),
        (row_block, col_block),
    )


def finish(gram_sum, running_r):
    total = (
        jnp.dot(
            running_r.T,
            running_r,
            precision=lax.Precision.HIGHEST,
            preferred_element_type=jnp.float32,
        )
        + gram_sum
    )
    return slice_out(lax.linalg.cholesky(total.T, symmetrize_input=False).T)


def plain(fields, x_factor, running_r):
    exchanged = lax.all_to_all(fields, "gx", split_axis=2, concat_axis=0, tiled=True)
    full_x, middle, part_cells = exchanged.shape
    product = lax.dot_general(
        x_factor,
        exchanged.reshape(full_x, middle * part_cells),
        (((0,), (0,)), ((), ())),
        preferred_element_type=jnp.float32,
    )
    projected = product.astype(jnp.bfloat16).reshape(x_factor.shape[1], middle, part_cells)
    fibres = lax.all_to_all(projected, "gy", split_axis=2, concat_axis=1, tiled=True)
    local_gram = lax.dot_general(
        fibres, fibres, (((0, 2), (0, 2)), ((), ())), preferred_element_type=jnp.float32
    )
    return finish(lax.psum(local_gram, ("gx", "gy")), running_r)


def pipelined(fields, x_factor, running_r):
    n_x, n_y = lax.axis_size("gx"), lax.axis_size("gy")
    me_x, me_y = lax.axis_index("gx"), lax.axis_index("gy")
    depth, rows, cells = fields.shape
    rank = x_factor.shape[1]
    share = rank // n_y
    cells_part = cells // n_x
    pieces = y_pieces(rows)
    by_y = jnp.transpose(fields, (1, 0, 2))

    factor = jnp.stack(
        [
            lax.dynamic_slice(x_factor, ((me_x ^ d) * depth, 0), (depth, rank)).T
            for d in range(n_x)
        ]
    )
    slow = n_y // 2
    shifts = [(dz, dy) for dz in range(slow) for dy in range(2)]

    def to(index, shift):
        return (index // 2 + shift[0]) % slow * 2 + (index % 2 + shift[1]) % 2

    def back(index, shift):
        return (index // 2 + slow - shift[0]) % slow * 2 + (index % 2 + shift[1]) % 2

    sends = jnp.stack([to(me_y, s) * share for s in shifts]).astype(jnp.int32)
    sources = jnp.stack([back(me_y, s) for s in shifts]).astype(jnp.int32)

    carried = None
    for k in range(cells_part // LANES):
        scalars = jnp.concatenate(
            [(me_x * cells_part + k * LANES).astype(jnp.int32)[None], sends]
        )
        blocks = [None] * (len(shifts) * len(pieces))
        for index, piece in enumerate(pieces):
            start, main, left = piece
            got = []
            for d in range(1, n_x):
                block = lax.dynamic_slice(
                    by_y,
                    (start, 0, (me_x ^ d) * cells_part + k * LANES),
                    (main + left, depth, LANES),
                )
                got.append(lax.ppermute(block, "gx", [(i, i ^ d) for i in range(n_x)]))
            outs = project(by_y, got, factor, scalars, piece, share)
            for part, shift in enumerate(shifts):
                block = outs[part]
                if shift != (0, 0):
                    block = lax.ppermute(block, "gy", [(i, to(i, shift)) for i in range(n_y)])
                blocks[part * len(pieces) + index] = block
        carried = gram(blocks, carried, sources, pieces, share)

    parts = n_y
    gram_sum = carried.reshape(parts, PITCH, parts, PITCH)[:, :rows, :, :rows]
    gram_sum = lax.psum(gram_sum.reshape(parts * rows, parts * rows), ("gx", "gy"))
    return finish(gram_sum, running_r)


def on_device(fields, x_factor, running_r):
    n_x, n_y = lax.axis_size("gx"), lax.axis_size("gy")
    depth, rows, cells = fields.shape
    rank = x_factor.shape[1]
    fits = (
        cells % (n_x * LANES) == 0
        and rank % (2 * n_y) == 0
        and depth % 8 == 0
        and 16 <= rows <= PITCH
        and rows % 16 in (0, 4, 8)
        and n_x & (n_x - 1) == 0
        and n_y % 2 == 0
        and n_y * PITCH % 256 == 0
    )
    if fits:
        return pipelined(fields, x_factor, running_r)
    return plain(fields, x_factor, running_r)


def solution(mesh):
    in_specs = (P("gx", "gy", None), P(), P())
    out_specs = P("gy", "gx")
    return jax.shard_map(
        on_device, mesh=mesh, in_specs=in_specs, out_specs=out_specs, check_vma=False
    )
```

```python
import functools

import jax
import jax.numpy as jnp
from jax import lax
from jax.experimental import pallas as pl
from jax.experimental.pallas import tpu as pltpu
from jax.sharding import PartitionSpec as P

LANES = 128
PITCH = 96
STEP = 256
VMEM_BYTES = 56 * 1024 * 1024


def y_pieces(rows):
    leftover = rows % 16
    main = rows - leftover
    pieces = []
    start = 0
    while start < main:
        size = min(32, main - start)
        pieces.append([start, size, 0])
        start += size
    pieces[-1][2] = leftover
    return [tuple(p) for p in pieces]


def pack_copies(fields, sends, scalars, cell, piece, sems):
    start, main, left = piece
    copies = []
    for index, send in enumerate(sends):
        column = pl.multiple_of(scalars[1 + index] + cell, LANES)
        copies.append(
            pltpu.make_async_copy(
                fields.at[pl.ds(start, main + left), :, pl.ds(column, LANES)],
                send,
                sems.at[index],
            )
        )
    return copies


def pack(fields, scalars, chunks, n_x):
    depth = fields.shape[1]
    n_sends = n_x - 1

    def body(scalars, fields, *rest):
        sems = rest[-1]
        copies = []
        for index, (cell, piece) in enumerate(chunks):
            sends = rest[index * n_sends : (index + 1) * n_sends]
            copies += pack_copies(fields, sends, scalars, cell, piece, sems.at[index])
        for copy in copies:
            copy.start()
        for copy in copies:
            copy.wait()

    any_space = pl.BlockSpec(memory_space=pl.ANY)
    shapes = [
        jax.ShapeDtypeStruct((piece[1] + piece[2], depth, LANES), jnp.bfloat16)
        for _, piece in chunks
        for _ in range(n_sends)
    ]
    outs = pl.pallas_call(
        body,
        out_shape=shapes,
        in_specs=[pl.BlockSpec(memory_space=pltpu.SMEM), any_space],
        out_specs=[any_space] * len(shapes),
        scratch_shapes=[pltpu.SemaphoreType.DMA((len(chunks), n_sends))],
        cost_estimate=pl.CostEstimate(flops=0, bytes_accessed=0, transcendentals=0),
        name="pack",
    )(scalars, fields)
    return [outs[i * n_sends : (i + 1) * n_sends] for i in range(len(chunks))]


def project_kernel(chunk, following, rank, share, scalars, fields, got, factor, outs, sends, own, wide, sems):
    cell, (start, main, left) = chunk
    rows = main + left
    column = pl.multiple_of(scalars[0] + cell, LANES)
    copy = pltpu.make_async_copy(
        fields.at[pl.ds(start, rows), :, pl.ds(column, LANES)], own, sems.at[0]
    )
    copy.start()
    packing = []
    if following is not None:
        packing = pack_copies(
            fields, sends, scalars, following[0], following[1], sems.at[pl.ds(1, len(sends))]
        )
    for other in packing:
        other.start()
    copy.wait()
    blocks = [own] + list(got)
    many = 4

    def one_group(group, _):
        y = group * many
        total = None
        for index, block in enumerate(blocks):
            right = jnp.concatenate([block[y + k] for k in range(many)], axis=1)
            term = jnp.dot(factor[index], right, preferred_element_type=jnp.float32)
            total = term if total is None else total + term
        for k in range(many):
            at = pl.multiple_of((y + k) * rank, 8)
            wide[pl.ds(at, rank), :] = total[:, k * LANES : (k + 1) * LANES]
        return 0

    lax.fori_loop(0, rows // many, one_group, 0)

    for part, out in enumerate(outs):
        first = scalars[1 + len(blocks) - 1 + part]

        def one_row(i, _):
            picked = wide[pl.ds(first + i, main, stride=rank), :]
            out[pl.ds(pl.multiple_of(i * main, 16), main), :] = picked.astype(jnp.bfloat16)
            return 0

        lax.fori_loop(0, share, one_row, 0, unroll=6)
        if left:
            per = 16 // left
            for group in range(0, share, per):
                count = min(per, share - group)
                tile = [
                    wide[pl.ds(main * rank + first + group + k, left, stride=rank), :]
                    for k in range(count)
                ]
                tile = jnp.concatenate(tile, axis=0).astype(jnp.bfloat16)
                at = share * main + group * left
                out[at : at + count * left, :] = tile
    for other in packing:
        other.wait()


def project(fields, got, factor, scalars, chunk, following, share, parts, after):
    _, (start, main, left) = chunk
    rows = main + left
    rank = factor.shape[1]
    depth = fields.shape[1]
    n_got = len(got)
    n_sends = 0 if following is None else n_got
    n_after = len(after)

    def body(scalars, fields, *rest):
        got = rest[:n_got]
        factor = rest[n_got]
        rest = rest[n_got + 1 + n_after :]
        outs = rest[:parts]
        sends = rest[parts : parts + n_sends]
        own, wide, sems = rest[parts + n_sends :]
        project_kernel(
            chunk, following, rank, share, scalars, fields, got, factor, outs, sends, own, wide, sems
        )

    vmem = pl.BlockSpec(memory_space=pltpu.VMEM)
    any_space = pl.BlockSpec(memory_space=pl.ANY)
    shapes = [jax.ShapeDtypeStruct((share * rows, LANES), jnp.bfloat16)] * parts
    if following is not None:
        next_rows = following[1][1] + following[1][2]
        shapes += [jax.ShapeDtypeStruct((next_rows, depth, LANES), jnp.bfloat16)] * n_sends
    outs = pl.pallas_call(
        body,
        out_shape=shapes,
        in_specs=[pl.BlockSpec(memory_space=pltpu.SMEM), any_space]
        + [vmem] * (n_got + 1)
        + [any_space] * n_after,
        out_specs=[vmem] * parts + [any_space] * n_sends,
        scratch_shapes=[
            pltpu.VMEM((rows, depth, LANES), jnp.bfloat16),
            pltpu.VMEM((rows * rank, LANES), jnp.float32),
            pltpu.SemaphoreType.DMA((1 + n_got,)),
        ],
        compiler_params=pltpu.CompilerParams(vmem_limit_bytes=VMEM_BYTES),
        cost_estimate=pl.CostEstimate(flops=0, bytes_accessed=0, transcendentals=0),
        name="project",
    )(scalars, fields, *got, factor, *after)
    return outs[:parts], outs[parts:]


def block_pairs(whole):
    return [(i, j) for i in range(0, whole, STEP) for j in range(i, whole, STEP)]


def gram_kernel(pieces, share, sources, blocks, carried, out, fibres):
    n_pieces = len(pieces)
    parts = len(blocks) // n_pieces
    whole = fibres.shape[0]

    for part in range(parts):
        base = pl.multiple_of(sources[part] * PITCH, 16)

        def one_row(i, _):
            at = pl.multiple_of(i * LANES, LANES)
            for index, (start, main, _left) in enumerate(pieces):
                block = blocks[part * n_pieces + index]
                fibres[pl.ds(base + start, main), pl.ds(at, LANES)] = block[
                    pl.ds(pl.multiple_of(i * main, 16), main), :
                ]
            return 0

        lax.fori_loop(0, share, one_row, 0)
        for index, (start, main, left) in enumerate(pieces):
            if not left:
                continue
            block = blocks[part * n_pieces + index]
            per = 16 // left
            for group in range(0, share, per):
                count = min(per, share - group)
                at = share * main + group * left
                tile = block[at : at + count * left, :].astype(jnp.float32)
                for k in range(count):
                    rows = tile[k * left : (k + 1) * left, :]
                    rows = jnp.concatenate(
                        [rows, jnp.zeros((16 - left, LANES), jnp.float32)], axis=0
                    )
                    fibres[
                        pl.ds(base + start + main, 16), (group + k) * LANES : (group + k + 1) * LANES
                    ] = rows.astype(jnp.bfloat16)

    at = 0
    for i, j in block_pairs(whole):
        product = lax.dot_general(
            fibres[i : i + STEP, :],
            fibres[j : j + STEP, :],
            (((1,), (1,)), ((), ())),
            preferred_element_type=jnp.float32,
        )
        if carried is not None:
            product = product + carried[at : at + STEP, :]
        out[at : at + STEP, :] = product
        at += STEP


def gram(blocks, carried, sources, pieces, share):
    parts = sources.shape[0]
    whole = parts * PITCH
    n_blocks = len(blocks)

    def body(sources, *rest):
        blocks = rest[:n_blocks]
        if carried is None:
            out, fibres = rest[n_blocks:]
            before = None
        else:
            before, out, fibres = rest[n_blocks:]
        gram_kernel(pieces, share, sources, blocks, before, out, fibres)

    vmem = pl.BlockSpec(memory_space=pltpu.VMEM)
    extra = [] if carried is None else [carried]
    return pl.pallas_call(
        body,
        out_shape=jax.ShapeDtypeStruct((len(block_pairs(whole)) * STEP, STEP), jnp.float32),
        in_specs=[pl.BlockSpec(memory_space=pltpu.SMEM)] + [vmem] * (n_blocks + len(extra)),
        out_specs=vmem,
        scratch_shapes=[pltpu.VMEM((whole, share * LANES), jnp.bfloat16)],
        compiler_params=pltpu.CompilerParams(vmem_limit_bytes=VMEM_BYTES),
        cost_estimate=pl.CostEstimate(flops=0, bytes_accessed=0, transcendentals=0),
        name="gram",
    )(sources, *blocks, *extra)


def slice_out(upper_r):
    row_block = upper_r.shape[0] // lax.axis_size("gy")
    col_block = upper_r.shape[1] // lax.axis_size("gx")
    return lax.dynamic_slice(
        upper_r,
        (lax.axis_index("gy") * row_block, lax.axis_index("gx") * col_block),
        (row_block, col_block),
    )


def finish(gram_sum, running_r):
    total = (
        jnp.dot(
            running_r.T,
            running_r,
            precision=lax.Precision.HIGHEST,
            preferred_element_type=jnp.float32,
        )
        + gram_sum
    )
    return slice_out(lax.linalg.cholesky(total.T, symmetrize_input=False).T)


def plain(fields, x_factor, running_r):
    exchanged = lax.all_to_all(fields, "gx", split_axis=2, concat_axis=0, tiled=True)
    full_x, middle, part_cells = exchanged.shape
    product = lax.dot_general(
        x_factor,
        exchanged.reshape(full_x, middle * part_cells),
        (((0,), (0,)), ((), ())),
        preferred_element_type=jnp.float32,
    )
    projected = product.astype(jnp.bfloat16).reshape(x_factor.shape[1], middle, part_cells)
    fibres = lax.all_to_all(projected, "gy", split_axis=2, concat_axis=1, tiled=True)
    local_gram = lax.dot_general(
        fibres, fibres, (((0, 2), (0, 2)), ((), ())), preferred_element_type=jnp.float32
    )
    return finish(lax.psum(local_gram, ("gx", "gy")), running_r)


def bit_of(axis, bit):
    return (lax.axis_index(axis) >> bit) & 1


def swap(value, axis, bit):
    flips = [(i, i ^ (1 << bit)) for i in range(lax.axis_size(axis))]
    return lax.ppermute(value, axis, flips)


def halve(value, axis, bit):
    halves = value.reshape(2, value.shape[0] // 2, value.shape[1])
    mine = bit_of(axis, bit)
    keep = lax.dynamic_index_in_dim(halves, mine, 0, keepdims=False)
    give = lax.dynamic_index_in_dim(halves, 1 - mine, 0, keepdims=False)
    return keep + swap(give, axis, bit)


def double(value, axis, bit):
    other = swap(value, axis, bit)
    return jnp.where(
        bit_of(axis, bit) == 0,
        jnp.concatenate([value, other]),
        jnp.concatenate([other, value]),
    )


def shift_slow(value, step, slow):
    n = slow * 2
    return lax.ppermute(value, "gy", [(i, (i + 2 * step) % n) for i in range(n)])


def sum_over_all(value):
    n_x, n_y = lax.axis_size("gx"), lax.axis_size("gy")
    bits = n_x.bit_length() - 1
    slow = n_y // 2
    mine = lax.axis_index("gy") // 2
    for bit in range(bits):
        value = halve(value, "gx", bit)
    value = halve(value, "gy", 0)
    rows, width = value.shape[0] // slow, value.shape[1]
    quarters = value.reshape(slow, rows, width)
    total = lax.dynamic_index_in_dim(quarters, mine, 0, keepdims=False)
    for step in range(1, slow):
        give = lax.dynamic_index_in_dim(quarters, (mine + step) % slow, 0, keepdims=False)
        total = total + shift_slow(give, step, slow)
    whole = jnp.zeros((slow, rows, width), value.dtype)
    whole = lax.dynamic_update_index_in_dim(whole, total, mine, 0)
    for step in range(1, slow):
        got = shift_slow(total, step, slow)
        whole = lax.dynamic_update_index_in_dim(whole, got, (mine + slow - step) % slow, 0)
    value = whole.reshape(slow * rows, width)
    value = double(value, "gy", 0)
    for bit in reversed(range(bits)):
        value = double(value, "gx", bit)
    return value


def pipelined(fields, x_factor, running_r):
    n_x, n_y = lax.axis_size("gx"), lax.axis_size("gy")
    me_x, me_y = lax.axis_index("gx"), lax.axis_index("gy")
    depth, rows, cells = fields.shape
    rank = x_factor.shape[1]
    share = rank // n_y
    cells_part = cells // n_x
    pieces = y_pieces(rows)
    by_y = jnp.transpose(fields, (1, 0, 2))

    factor = jnp.stack(
        [
            lax.dynamic_slice(x_factor, ((me_x ^ d) * depth, 0), (depth, rank)).T
            for d in range(n_x)
        ]
    )
    slow = n_y // 2
    shifts = [(dz, dy) for dz in range(slow) for dy in range(2)]

    def to(index, shift):
        return (index // 2 + shift[0]) % slow * 2 + (index % 2 + shift[1]) % 2

    def back(index, shift):
        return (index // 2 + slow - shift[0]) % slow * 2 + (index % 2 + shift[1]) % 2

    scalars = jnp.stack(
        [(me_x ^ d) * cells_part for d in range(n_x)] + [to(me_y, s) * share for s in shifts]
    ).astype(jnp.int32)
    sources = jnp.stack([back(me_y, s) for s in shifts]).astype(jnp.int32)

    chunks = [(cell, piece) for cell in range(0, cells_part, LANES) for piece in pieces]
    per_gram = len(pieces)

    def exchange_x(sends):
        return [
            lax.ppermute(send, "gx", [(i, i ^ (d + 1)) for i in range(n_x)])
            for d, send in enumerate(sends)
        ]

    ahead = 2
    moving = [exchange_x(sends) for sends in pack(by_y, scalars, chunks[:ahead], n_x)]
    arrived = []
    carried = None
    for k, chunk in enumerate(chunks):
        following = chunks[k + ahead] if k + ahead < len(chunks) else None
        after = []
        if k >= 2:
            after += arrived[k - 2][1:]
        if k >= per_gram + 2 and (k - 2) % per_gram == 0:
            after.append(carried)
        outs, sends = project(
            by_y, moving[k], factor, scalars, chunk, following, share, len(shifts), after
        )
        if following is not None:
            moving.append(exchange_x(sends))
        arrived.append(
            [
                out
                if shift == (0, 0)
                else lax.ppermute(out, "gy", [(i, to(i, shift)) for i in range(n_y)])
                for out, shift in zip(outs, shifts)
            ]
        )
        if (k + 1) % per_gram == 0:
            group = arrived[k + 1 - per_gram :]
            blocks = [group[index][part] for part in range(n_y) for index in range(per_gram)]
            carried = gram(blocks, carried, sources, pieces, share)

    summed = sum_over_all(carried)
    whole = n_y * PITCH
    blocks = {
        pair: summed[index * STEP : (index + 1) * STEP]
        for index, pair in enumerate(block_pairs(whole))
    }
    none = jnp.zeros((STEP, STEP), jnp.float32)
    starts = range(0, whole, STEP)
    upper = jnp.concatenate(
        [jnp.concatenate([blocks.get((i, j), none) for j in starts], axis=1) for i in starts]
    )
    gram_sum = upper.reshape(n_y, PITCH, n_y, PITCH)[:, :rows, :, :rows]
    return finish(gram_sum.reshape(n_y * rows, n_y * rows), running_r)


def on_device(fields, x_factor, running_r):
    n_x, n_y = lax.axis_size("gx"), lax.axis_size("gy")
    depth, rows, cells = fields.shape
    rank = x_factor.shape[1]
    fits = (
        cells % (n_x * LANES) == 0
        and rank % (2 * n_y) == 0
        and depth % 8 == 0
        and 16 <= rows <= PITCH
        and rows % 16 in (0, 4, 8)
        and n_x & (n_x - 1) == 0
        and n_y % 2 == 0
        and n_y * PITCH % STEP == 0
        and len(block_pairs(n_y * PITCH)) * STEP % (8 * n_x * n_y) == 0
    )
    if fits:
        return pipelined(fields, x_factor, running_r)
    return plain(fields, x_factor, running_r)


def solution(mesh):
    in_specs = (P("gx", "gy", None), P(), P())
    out_specs = P("gy", "gx")
    return jax.shard_map(
        on_device, mesh=mesh, in_specs=in_specs, out_specs=out_specs, check_vma=False
    )
```

```python
import functools

import jax
import jax.numpy as jnp
from jax import lax
from jax.experimental import pallas as pl
from jax.experimental.pallas import tpu as pltpu
from jax.sharding import PartitionSpec as P

LANES = 128
PITCH = 96
STEP = 256
WINDOW = {"gx": 3, "gy": 2}
AHEAD = 3
VMEM_BYTES = 56 * 1024 * 1024


def y_pieces(rows):
    leftover = rows % 16
    main = rows - leftover
    pieces = []
    start = 0
    while start < main:
        size = min(32, main - start)
        pieces.append([start, size, 0])
        start += size
    pieces[-1][2] = leftover
    return [tuple(p) for p in pieces]


def send_list(chunk, n_x):
    _, (_, main, left) = chunk
    rows = main + left
    return [(partner, 0, rows) for partner in list(range(2, n_x)) + [1]]


def pack_copies(fields, outs, scalars, chunk, n_x, sems):
    cell, (start, _, _) = chunk
    copies = []
    for index, (partner, at, size) in enumerate(send_list(chunk, n_x)):
        column = pl.multiple_of(scalars[partner] + cell, LANES)
        copies.append(
            pltpu.make_async_copy(
                fields.at[pl.ds(start + at, size), :, pl.ds(column, LANES)],
                outs[index],
                sems.at[index],
            )
        )
    return copies


def send_shapes(chunk, n_x, depth):
    return [
        jax.ShapeDtypeStruct((size, depth, LANES), jnp.bfloat16)
        for _, _, size in send_list(chunk, n_x)
    ]


def pack(fields, scalars, chunk, n_x):
    shapes = send_shapes(chunk, n_x, fields.shape[1])

    def body(scalars, fields, *rest):
        copies = pack_copies(fields, rest[:-1], scalars, chunk, n_x, rest[-1])
        for copy in copies:
            copy.start()
        for copy in copies:
            copy.wait()

    return pl.pallas_call(
        body,
        out_shape=shapes,
        in_specs=[pl.BlockSpec(memory_space=pltpu.SMEM), pl.BlockSpec(memory_space=pl.ANY)],
        out_specs=[pl.BlockSpec(memory_space=pltpu.VMEM)] * len(shapes),
        scratch_shapes=[pltpu.SemaphoreType.DMA((len(shapes),))],
        compiler_params=pltpu.CompilerParams(vmem_limit_bytes=VMEM_BYTES),
        cost_estimate=pl.CostEstimate(flops=0, bytes_accessed=0, transcendentals=0),
        name="pack",
    )(scalars, fields)


def project_kernel(chunk, following, n_x, rank, share, scalars, fields, got, factor, outs, sends, own, wide, sems):
    cell, (start, main, left) = chunk
    rows = main + left
    column = pl.multiple_of(scalars[0] + cell, LANES)
    copy = pltpu.make_async_copy(
        fields.at[pl.ds(start, rows), :, pl.ds(column, LANES)], own, sems.at[0]
    )
    copy.start()
    packing = []
    if following is not None:
        packing = pack_copies(
            fields, sends, scalars, following, n_x, sems.at[pl.ds(1, len(sends))]
        )
    for other in packing:
        other.start()
    copy.wait()
    many = 4
    arrays = list(zip(send_list(chunk, n_x), got))

    for start_row, size in sorted({(at, size) for (p, at, size), _ in arrays if p > 1}):
        blocks = [(0, own, 0)]
        for (partner, at, _), block in arrays:
            if partner == 1 or at == start_row:
                blocks.append((partner, block, at))

        def one_group(group, _):
            y = start_row + group * many
            total = None
            for partner, block, at in blocks:
                right = jnp.concatenate([block[y - at + k] for k in range(many)], axis=1)
                term = jnp.dot(factor[partner], right, preferred_element_type=jnp.float32)
                total = term if total is None else total + term
            for k in range(many):
                at = pl.multiple_of((y + k) * rank, 8)
                wide[pl.ds(at, rank), :] = total[:, k * LANES : (k + 1) * LANES]
            return 0

        lax.fori_loop(0, size // many, one_group, 0)

    for part, out in enumerate(outs):
        first = scalars[n_x + part]

        def one_row(i, _):
            picked = wide[pl.ds(first + i, main, stride=rank), :]
            out[pl.ds(pl.multiple_of(i * main, 16), main), :] = picked.astype(jnp.bfloat16)
            return 0

        lax.fori_loop(0, share, one_row, 0, unroll=6)
        if left:
            per = 16 // left
            for group in range(0, share, per):
                count = min(per, share - group)
                tile = [
                    wide[pl.ds(main * rank + first + group + k, left, stride=rank), :]
                    for k in range(count)
                ]
                tile = jnp.concatenate(tile, axis=0).astype(jnp.bfloat16)
                at = share * main + group * left
                out[at : at + count * left, :] = tile
    for other in packing:
        other.wait()


def project(fields, got, factor, scalars, chunk, following, n_x, share, parts, after):
    _, (start, main, left) = chunk
    rows = main + left
    rank = factor.shape[1]
    depth = fields.shape[1]
    n_got = len(got)
    n_sends = 0 if following is None else n_got
    vmem = pl.BlockSpec(memory_space=pltpu.VMEM)
    any_space = pl.BlockSpec(memory_space=pl.ANY)
    n_after = len(after)

    def body(scalars, fields, *rest):
        got = rest[:n_got]
        factor = rest[n_got]
        rest = rest[n_got + 1 + n_after :]
        outs = rest[:parts]
        sends = rest[parts : parts + n_sends]
        own, wide, sems = rest[parts + n_sends :]
        project_kernel(
            chunk, following, n_x, rank, share, scalars, fields, got, factor, outs, sends, own, wide, sems
        )

    shapes = [jax.ShapeDtypeStruct((share * rows, LANES), jnp.bfloat16)] * parts
    if following is not None:
        shapes += send_shapes(following, n_x, depth)
    outs = pl.pallas_call(
        body,
        out_shape=shapes,
        in_specs=[pl.BlockSpec(memory_space=pltpu.SMEM), any_space]
        + [vmem] * (n_got + 1)
        + [any_space] * n_after,
        out_specs=[vmem] * (parts + n_sends),
        scratch_shapes=[
            pltpu.VMEM((rows, depth, LANES), jnp.bfloat16),
            pltpu.VMEM((rows * rank, LANES), jnp.float32),
            pltpu.SemaphoreType.DMA((1 + n_got,)),
        ],
        compiler_params=pltpu.CompilerParams(vmem_limit_bytes=VMEM_BYTES),
        cost_estimate=pl.CostEstimate(flops=0, bytes_accessed=0, transcendentals=0),
        name="project",
    )(scalars, fields, *got, factor, *after)
    return outs[:parts], outs[parts:]


def block_pairs(whole):
    return [(i, j) for i in range(0, whole, STEP) for j in range(i, whole, STEP)]


def gram_kernel(pieces, share, sources, blocks, carried, out, fibres):
    n_pieces = len(pieces)
    parts = len(blocks) // n_pieces
    whole = fibres.shape[0]

    for part in range(parts):
        base = pl.multiple_of(sources[part] * PITCH, 16)

        def one_row(i, _):
            at = pl.multiple_of(i * LANES, LANES)
            for index, (start, main, _left) in enumerate(pieces):
                block = blocks[part * n_pieces + index]
                fibres[pl.ds(base + start, main), pl.ds(at, LANES)] = block[
                    pl.ds(pl.multiple_of(i * main, 16), main), :
                ]
            return 0

        lax.fori_loop(0, share, one_row, 0)
        for index, (start, main, left) in enumerate(pieces):
            if not left:
                continue
            block = blocks[part * n_pieces + index]
            per = 16 // left
            for group in range(0, share, per):
                count = min(per, share - group)
                at = share * main + group * left
                tile = block[at : at + count * left, :].astype(jnp.float32)
                for k in range(count):
                    rows = tile[k * left : (k + 1) * left, :]
                    rows = jnp.concatenate(
                        [rows, jnp.zeros((16 - left, LANES), jnp.float32)], axis=0
                    )
                    fibres[
                        pl.ds(base + start + main, 16), (group + k) * LANES : (group + k + 1) * LANES
                    ] = rows.astype(jnp.bfloat16)

    at = 0
    for i, j in block_pairs(whole):
        product = lax.dot_general(
            fibres[i : i + STEP, :],
            fibres[j : j + STEP, :],
            (((1,), (1,)), ((), ())),
            preferred_element_type=jnp.float32,
        )
        if carried is not None:
            product = product + carried[at : at + STEP, :]
        out[at : at + STEP, :] = product
        at += STEP


def gram(blocks, carried, sources, pieces, share):
    parts = sources.shape[0]
    whole = parts * PITCH
    n_blocks = len(blocks)

    def body(sources, *rest):
        blocks = rest[:n_blocks]
        if carried is None:
            out, fibres = rest[n_blocks:]
            before = None
        else:
            before, out, fibres = rest[n_blocks:]
        gram_kernel(pieces, share, sources, blocks, before, out, fibres)

    vmem = pl.BlockSpec(memory_space=pltpu.VMEM)
    extra = [] if carried is None else [carried]
    return pl.pallas_call(
        body,
        out_shape=jax.ShapeDtypeStruct((len(block_pairs(whole)) * STEP, STEP), jnp.float32),
        in_specs=[pl.BlockSpec(memory_space=pltpu.SMEM)] + [vmem] * (n_blocks + len(extra)),
        out_specs=vmem,
        scratch_shapes=[pltpu.VMEM((whole, share * LANES), jnp.bfloat16)],
        compiler_params=pltpu.CompilerParams(vmem_limit_bytes=VMEM_BYTES),
        cost_estimate=pl.CostEstimate(flops=0, bytes_accessed=0, transcendentals=0),
        name="gram",
    )(sources, *blocks, *extra)


def slice_out(upper_r):
    row_block = upper_r.shape[0] // lax.axis_size("gy")
    col_block = upper_r.shape[1] // lax.axis_size("gx")
    return lax.dynamic_slice(
        upper_r,
        (lax.axis_index("gy") * row_block, lax.axis_index("gx") * col_block),
        (row_block, col_block),
    )


def finish(gram_sum, running_r):
    total = (
        jnp.dot(
            running_r.T,
            running_r,
            precision=lax.Precision.HIGHEST,
            preferred_element_type=jnp.float32,
        )
        + gram_sum
    )
    return slice_out(lax.linalg.cholesky(total.T, symmetrize_input=False).T)


def plain(fields, x_factor, running_r):
    exchanged = lax.all_to_all(fields, "gx", split_axis=2, concat_axis=0, tiled=True)
    full_x, middle, part_cells = exchanged.shape
    product = lax.dot_general(
        x_factor,
        exchanged.reshape(full_x, middle * part_cells),
        (((0,), (0,)), ((), ())),
        preferred_element_type=jnp.float32,
    )
    projected = product.astype(jnp.bfloat16).reshape(x_factor.shape[1], middle, part_cells)
    fibres = lax.all_to_all(projected, "gy", split_axis=2, concat_axis=1, tiled=True)
    local_gram = lax.dot_general(
        fibres, fibres, (((0, 2), (0, 2)), ((), ())), preferred_element_type=jnp.float32
    )
    return finish(lax.psum(local_gram, ("gx", "gy")), running_r)


def bit_of(axis, bit):
    return (lax.axis_index(axis) >> bit) & 1


def swap(value, axis, bit):
    flips = [(i, i ^ (1 << bit)) for i in range(lax.axis_size(axis))]
    return lax.ppermute(value, axis, flips)


def halve(value, axis, bit):
    halves = value.reshape(2, value.shape[0] // 2, value.shape[1])
    mine = bit_of(axis, bit)
    keep = lax.dynamic_index_in_dim(halves, mine, 0, keepdims=False)
    give = lax.dynamic_index_in_dim(halves, 1 - mine, 0, keepdims=False)
    return keep + swap(give, axis, bit)


def double(value, axis, bit):
    other = swap(value, axis, bit)
    return jnp.where(
        bit_of(axis, bit) == 0,
        jnp.concatenate([value, other]),
        jnp.concatenate([other, value]),
    )


def shift_slow(value, step, slow):
    n = slow * 2
    return lax.ppermute(value, "gy", [(i, (i + 2 * step) % n) for i in range(n)])


def sum_over_all(value):
    n_x, n_y = lax.axis_size("gx"), lax.axis_size("gy")
    bits = n_x.bit_length() - 1
    slow = n_y // 2
    mine = lax.axis_index("gy") // 2
    for bit in range(bits):
        value = halve(value, "gx", bit)
    value = halve(value, "gy", 0)
    rows, width = value.shape[0] // slow, value.shape[1]
    quarters = value.reshape(slow, rows, width)
    total = lax.dynamic_index_in_dim(quarters, mine, 0, keepdims=False)
    for step in range(1, slow):
        give = lax.dynamic_index_in_dim(quarters, (mine + step) % slow, 0, keepdims=False)
        total = total + shift_slow(give, step, slow)
    whole = jnp.zeros((slow, rows, width), value.dtype)
    whole = lax.dynamic_update_index_in_dim(whole, total, mine, 0)
    for step in range(1, slow):
        got = shift_slow(total, step, slow)
        whole = lax.dynamic_update_index_in_dim(whole, got, (mine + slow - step) % slow, 0)
    value = whole.reshape(slow * rows, width)
    value = double(value, "gy", 0)
    for bit in reversed(range(bits)):
        value = double(value, "gx", bit)
    return value


def pipelined(fields, x_factor, running_r):
    n_x, n_y = lax.axis_size("gx"), lax.axis_size("gy")
    me_x, me_y = lax.axis_index("gx"), lax.axis_index("gy")
    depth, rows, cells = fields.shape
    rank = x_factor.shape[1]
    share = rank // n_y
    cells_part = cells // n_x
    pieces = y_pieces(rows)
    by_y = jnp.transpose(fields, (1, 0, 2))

    factor = jnp.stack(
        [
            lax.dynamic_slice(x_factor, ((me_x ^ d) * depth, 0), (depth, rank)).T
            for d in range(n_x)
        ]
    )
    slow = n_y // 2
    shifts = [(dz, dy) for dz in range(slow) for dy in range(2)]

    def to(index, shift):
        return (index // 2 + shift[0]) % slow * 2 + (index % 2 + shift[1]) % 2

    def back(index, shift):
        return (index // 2 + slow - shift[0]) % slow * 2 + (index % 2 + shift[1]) % 2

    scalars = jnp.stack(
        [(me_x ^ d) * cells_part for d in range(n_x)] + [to(me_y, s) * share for s in shifts]
    ).astype(jnp.int32)
    sources = jnp.stack([back(me_y, s) for s in shifts]).astype(jnp.int32)

    chunks = [(cell, piece) for cell in range(0, cells_part, LANES) for piece in pieces]
    per_gram = len(pieces)

    flown = []
    lanes = {"gx": [], "gy": []}

    def start(operand, axis, pairs):
        lane = lanes[axis]
        if len(lane) >= WINDOW[axis]:
            slot = lane[-WINDOW[axis]]
            operand, flown[slot] = lax.optimization_barrier((operand, flown[slot]))
        lane.append(len(flown))
        flown.append(lax.ppermute(operand, axis, pairs))
        return lane[-1]

    def start_x(chunk, sends):
        return [
            functools.partial(start, send, "gx", [(i, i ^ partner) for i in range(n_x)])
            for (partner, _, _), send in zip(send_list(chunk, n_x), sends)
        ]

    def start_y(outs):
        return [
            functools.partial(start, out, "gy", [(i, to(i, shift)) for i in range(n_y)])
            for out, shift in zip(outs, shifts)
            if shift != (0, 0)
        ]

    moving = []
    for chunk in chunks[:AHEAD]:
        moving.append([begin() for begin in start_x(chunk, pack(by_y, scalars, chunk, n_x))])
    arrived = []
    carried = None

    def add_gram(carried, group):
        blocks = []
        for part in range(n_y):
            for own, slots in group:
                blocks.append(own if part == 0 else flown[slots[part - 1]])
        return gram(blocks, carried, sources, pieces, share)

    for k, chunk in enumerate(chunks):
        following = chunks[k + AHEAD] if k + AHEAD < len(chunks) else None
        after = []
        if k >= per_gram + 2 and (k - 2) % per_gram == 0:
            done = k - 2 - per_gram
            carried = add_gram(carried, arrived[done : done + per_gram])
            after.append(carried)
        got = [flown[slot] for slot in moving[k]]
        outs, sends = project(
            by_y, got, factor, scalars, chunk, following, n_x, share, len(shifts), after
        )
        to_y = start_y(outs)
        to_x = [] if following is None else start_x(following, sends)
        order = sorted(
            [((i + 0.5) / len(to_y), 0, i) for i in range(len(to_y))]
            + [((i + 0.25) / len(to_x), 1, i) for i in range(len(to_x))]
        )
        slots = [[None] * len(to_y), [None] * len(to_x)]
        for _, which, i in order:
            slots[which][i] = (to_y, to_x)[which][i]()
        arrived.append((outs[0], slots[0]))
        if following is not None:
            moving.append(slots[1])
    for done in range(0, len(chunks), per_gram):
        if done + per_gram + 2 >= len(chunks):
            carried = add_gram(carried, arrived[done : done + per_gram])

    summed = sum_over_all(carried)
    whole = n_y * PITCH
    blocks = {
        pair: summed[index * STEP : (index + 1) * STEP]
        for index, pair in enumerate(block_pairs(whole))
    }
    none = jnp.zeros((STEP, STEP), jnp.float32)
    starts = range(0, whole, STEP)
    upper = jnp.concatenate(
        [jnp.concatenate([blocks.get((i, j), none) for j in starts], axis=1) for i in starts]
    )
    gram_sum = upper.reshape(n_y, PITCH, n_y, PITCH)[:, :rows, :, :rows]
    return finish(gram_sum.reshape(n_y * rows, n_y * rows), running_r)


def on_device(fields, x_factor, running_r):
    n_x, n_y = lax.axis_size("gx"), lax.axis_size("gy")
    depth, rows, cells = fields.shape
    rank = x_factor.shape[1]
    fits = (
        cells % (n_x * LANES) == 0
        and rank % (2 * n_y) == 0
        and depth % 8 == 0
        and 16 <= rows <= PITCH
        and rows % 16 in (0, 4, 8)
        and n_x & (n_x - 1) == 0
        and n_y % 2 == 0
        and n_y * PITCH % STEP == 0
        and len(block_pairs(n_y * PITCH)) * STEP % (8 * n_x * n_y) == 0
    )
    if fits:
        return pipelined(fields, x_factor, running_r)
    return plain(fields, x_factor, running_r)


def solution(mesh):
    in_specs = (P("gx", "gy", None), P(), P())
    out_specs = P("gy", "gx")
    return jax.shard_map(
        on_device, mesh=mesh, in_specs=in_specs, out_specs=out_specs, check_vma=False
    )
```

```python
import functools

import jax
import jax.numpy as jnp
from jax import lax
from jax.experimental import pallas as pl
from jax.experimental.pallas import tpu as pltpu
from jax.sharding import PartitionSpec as P

LANES = 128
SUB = 32
STEP = 256
WINDOW = 5
AHEAD = 2
VMEM_BYTES = 56 * 1024 * 1024


def y_pieces(rows):
    count = -(-rows // SUB)
    size = rows // count
    return [(i * size, size) for i in range(count)]


def pitch_of(rows):
    return len(y_pieces(rows)) * SUB


def send_list(chunk, n_x):
    rows = chunk[1][1]
    half = rows // 2
    return [(partner, at, half) for at in (0, half) for partner in range(2, n_x)]


def copy_cells(fields, out, scalars, partner, cell, start, size, sem):
    column = pl.multiple_of(scalars[partner] + cell, LANES)
    return pltpu.make_async_copy(
        fields.at[pl.ds(start, size), :, pl.ds(column, LANES)], out, sem
    )


def chunk_copies(fields, outs, scalars, chunk, n_x, sems):
    cell, (start, _) = chunk
    return [
        copy_cells(fields, outs[i], scalars, partner, cell, start + at, size, sems.at[i])
        for i, (partner, at, size) in enumerate(send_list(chunk, n_x))
    ]


def run_pack(fields, scalars, shapes, make_copies):
    def body(scalars, fields, *rest):
        copies = make_copies(fields, rest[:-1], scalars, rest[-1])
        for copy in copies:
            copy.start()
        for copy in copies:
            copy.wait()

    return pl.pallas_call(
        body,
        out_shape=shapes,
        in_specs=[pl.BlockSpec(memory_space=pltpu.SMEM), pl.BlockSpec(memory_space=pl.ANY)],
        out_specs=[pl.BlockSpec(memory_space=pltpu.VMEM)] * len(shapes),
        scratch_shapes=[pltpu.SemaphoreType.DMA((len(shapes),))],
        compiler_params=pltpu.CompilerParams(vmem_limit_bytes=VMEM_BYTES),
        cost_estimate=pl.CostEstimate(flops=0, bytes_accessed=0, transcendentals=0),
        name="pack",
    )(scalars, fields)


def send_shapes(chunk, n_x, depth):
    return [
        jax.ShapeDtypeStruct((size, depth, LANES), jnp.bfloat16)
        for _, _, size in send_list(chunk, n_x)
    ]


def pack(fields, scalars, chunk, n_x):
    return run_pack(
        fields,
        scalars,
        send_shapes(chunk, n_x, fields.shape[1]),
        lambda fields, outs, scalars, sems: chunk_copies(fields, outs, scalars, chunk, n_x, sems),
    )


def pack_near(fields, scalars, cell):
    rows, depth = fields.shape[:2]
    return run_pack(
        fields,
        scalars,
        [jax.ShapeDtypeStruct((rows, depth, LANES), jnp.bfloat16)],
        lambda fields, outs, scalars, sems: [
            copy_cells(fields, outs[0], scalars, 1, cell, 0, rows, sems.at[0])
        ],
    )[0]


def project_kernel(chunk, following, n_x, rank, share, scalars, fields, near, got, factor, outs, sends, own, other, wide, sems):
    cell, (start, rows) = chunk
    copies = [
        copy_cells(fields, own, scalars, 0, cell, start, rows, sems.at[0]),
        pltpu.make_async_copy(near.at[pl.ds(start, rows)], other, sems.at[1]),
    ]
    for copy in copies:
        copy.start()
    packing = []
    if following is not None:
        packing = chunk_copies(
            fields, sends, scalars, following, n_x, sems.at[pl.ds(2, len(sends))]
        )
    for copy in packing:
        copy.start()
    for copy in copies:
        copy.wait()

    half = rows // 2
    many = max(n for n in range(1, 9) if half % n == 0)
    for start_row in (0, half):
        blocks = [(0, own, 0), (1, other, 0)]
        for (partner, at, _), block in zip(send_list(chunk, n_x), got):
            if at == start_row:
                blocks.append((partner, block, at))

        def one_group(group, _):
            y = start_row + group * many
            total = None
            for partner, block, at in blocks:
                right = jnp.concatenate([block[y - at + k] for k in range(many)], axis=1)
                term = jnp.dot(factor[partner], right, preferred_element_type=jnp.float32)
                total = term if total is None else total + term
            for k in range(many):
                at = pl.multiple_of((y + k) * rank, 8)
                wide[pl.ds(at, rank), :] = total[:, k * LANES : (k + 1) * LANES]
            return 0

        lax.fori_loop(0, half // many, one_group, 0)

    main = rows // 16 * 16
    left = rows - main
    for part in range(2 * len(outs)):
        out = outs[part // 2].at[part % 2]
        first = scalars[n_x + part]

        def one_row(i, _):
            picked = wide[pl.ds(first + i, main, stride=rank), :]
            out[pl.ds(pl.multiple_of(i * main, 16), main), :] = picked.astype(jnp.bfloat16)
            return 0

        lax.fori_loop(0, share, one_row, 0, unroll=6)
        for group in range(0, share if left else 0, 4):
            count = min(4, share - group)
            tile = [
                wide[pl.ds(main * rank + first + group + k, left, stride=rank), :]
                for k in range(count)
            ]
            tile = jnp.concatenate(tile, axis=0).astype(jnp.bfloat16)
            at = share * main + group * left
            out[at : at + count * left, :] = tile
    for copy in packing:
        copy.wait()


def project(fields, near, got, factor, scalars, chunk, following, n_x, share, slow, after):
    rows = chunk[1][1]
    rank = factor.shape[1]
    depth = fields.shape[1]
    n_got = len(got)
    n_sends = 0 if following is None else n_got
    n_after = len(after)
    vmem = pl.BlockSpec(memory_space=pltpu.VMEM)
    any_space = pl.BlockSpec(memory_space=pl.ANY)

    def body(scalars, fields, near, *rest):
        got = rest[:n_got]
        factor = rest[n_got]
        rest = rest[n_got + 1 + n_after :]
        outs = rest[:slow]
        sends = rest[slow : slow + n_sends]
        own, other, wide, sems = rest[slow + n_sends :]
        project_kernel(
            chunk, following, n_x, rank, share, scalars, fields, near, got, factor, outs, sends, own, other, wide, sems
        )

    shapes = [jax.ShapeDtypeStruct((2, share * rows, LANES), jnp.bfloat16)] * slow
    if following is not None:
        shapes += send_shapes(following, n_x, depth)
    outs = pl.pallas_call(
        body,
        out_shape=shapes,
        in_specs=[pl.BlockSpec(memory_space=pltpu.SMEM), any_space, any_space]
        + [vmem] * (n_got + 1)
        + [any_space] * n_after,
        out_specs=[vmem] * (slow + n_sends),
        scratch_shapes=[
            pltpu.VMEM((rows, depth, LANES), jnp.bfloat16),
            pltpu.VMEM((rows, depth, LANES), jnp.bfloat16),
            pltpu.VMEM((rows * rank, LANES), jnp.float32),
            pltpu.SemaphoreType.DMA((2 + n_got,)),
        ],
        compiler_params=pltpu.CompilerParams(vmem_limit_bytes=VMEM_BYTES),
        cost_estimate=pl.CostEstimate(flops=0, bytes_accessed=0, transcendentals=0),
        name="project",
    )(scalars, fields, near, *got, factor, *after)
    return outs[:slow], outs[slow:]


def block_pairs(whole):
    return [(i, j) for i in range(0, whole, STEP) for j in range(i, whole, STEP)]


def gram_kernel(pieces, share, places, blocks, carried, out, fibres):
    whole = fibres.shape[0]
    rows = pieces[0][1]
    main = rows // 16 * 16
    left = rows - main

    for place, block in zip(places, blocks):
        base = pl.multiple_of(place, 16)

        def one_row(i, _):
            at = pl.multiple_of(i * LANES, LANES)
            fibres[pl.ds(base, main), pl.ds(at, LANES)] = block[
                pl.ds(pl.multiple_of(i * main, 16), main), :
            ]
            return 0

        lax.fori_loop(0, share, one_row, 0, unroll=6)
        for group in range(0, share if left else 0, 4):
            count = min(4, share - group)
            at = share * main + group * left
            tile = block[at : at + count * left, :].astype(jnp.float32)
            for k in range(count):
                part = tile[k * left : (k + 1) * left, :]
                part = jnp.concatenate([part, jnp.zeros((16 - left, LANES), jnp.float32)], axis=0)
                fibres[
                    pl.ds(base + main, 16), (group + k) * LANES : (group + k + 1) * LANES
                ] = part.astype(jnp.bfloat16)

    at = 0
    for i, j in block_pairs(whole):
        product = lax.dot_general(
            fibres[i : i + STEP, :],
            fibres[j : j + STEP, :],
            (((1,), (1,)), ((), ())),
            preferred_element_type=jnp.float32,
        )
        if carried is not None:
            product = product + carried[at : at + STEP, :]
        out[at : at + STEP, :] = product
        at += STEP


def gram(straight, crossed, carried, sources, pieces, share):
    count = len(pieces)
    slow = len(straight[0])
    pitch = count * SUB
    whole = 2 * slow * pitch
    inputs = [block for piece in straight for block in piece]
    inputs += [block for piece in crossed for block in piece]
    size = inputs[0].shape[1]

    def body(sources, *rest):
        blocks, places = [], []
        refs = list(rest[: len(inputs)])
        for i in range(count):
            for dz in range(slow):
                blocks.append(refs.pop(0).at[0])
                places.append(sources[2 * dz] * pitch + i * SUB)
        for i in range(count):
            for j in range(slow // 2):
                ref = refs.pop(0)
                for k in range(2):
                    blocks.append(ref.at[k])
                    places.append(sources[2 * (2 * j + k) + 1] * pitch + i * SUB)
        if carried is None:
            out, fibres = rest[len(inputs) :]
            before = None
        else:
            before, out, fibres = rest[len(inputs) :]
        gram_kernel(pieces, share, places, blocks, before, out, fibres)

    half = pl.BlockSpec((1, size, LANES), lambda i: (0, 0, 0))
    both = pl.BlockSpec((2, size, LANES), lambda i: (0, 0, 0))
    shape = (len(block_pairs(whole)) * STEP, STEP)
    square = pl.BlockSpec(shape, lambda i: (0, 0))
    extra = [] if carried is None else [carried]
    return pl.pallas_call(
        body,
        grid=(1,),
        out_shape=jax.ShapeDtypeStruct(shape, jnp.float32),
        in_specs=[pl.BlockSpec(memory_space=pltpu.SMEM)]
        + [half] * (count * slow)
        + [both] * (count * slow // 2)
        + [square] * len(extra),
        out_specs=square,
        scratch_shapes=[pltpu.VMEM((whole, share * LANES), jnp.bfloat16)],
        compiler_params=pltpu.CompilerParams(vmem_limit_bytes=VMEM_BYTES),
        cost_estimate=pl.CostEstimate(flops=0, bytes_accessed=0, transcendentals=0),
        name="gram",
    )(sources, *inputs, *extra)


def slice_out(upper_r):
    row_block = upper_r.shape[0] // lax.axis_size("gy")
    col_block = upper_r.shape[1] // lax.axis_size("gx")
    return lax.dynamic_slice(
        upper_r,
        (lax.axis_index("gy") * row_block, lax.axis_index("gx") * col_block),
        (row_block, col_block),
    )


def finish(gram_sum, running_r):
    total = (
        jnp.dot(
            running_r.T,
            running_r,
            precision=lax.Precision.HIGHEST,
            preferred_element_type=jnp.float32,
        )
        + gram_sum
    )
    return slice_out(lax.linalg.cholesky(total.T, symmetrize_input=False).T)


def plain(fields, x_factor, running_r):
    exchanged = lax.all_to_all(fields, "gx", split_axis=2, concat_axis=0, tiled=True)
    full_x, middle, part_cells = exchanged.shape
    product = lax.dot_general(
        x_factor,
        exchanged.reshape(full_x, middle * part_cells),
        (((0,), (0,)), ((), ())),
        preferred_element_type=jnp.float32,
    )
    projected = product.astype(jnp.bfloat16).reshape(x_factor.shape[1], middle, part_cells)
    fibres = lax.all_to_all(projected, "gy", split_axis=2, concat_axis=1, tiled=True)
    local_gram = lax.dot_general(
        fibres, fibres, (((0, 2), (0, 2)), ((), ())), preferred_element_type=jnp.float32
    )
    return finish(lax.psum(local_gram, ("gx", "gy")), running_r)


def bit_of(axis, bit):
    return (lax.axis_index(axis) >> bit) & 1


def swap(value, axis, bit):
    flips = [(i, i ^ (1 << bit)) for i in range(lax.axis_size(axis))]
    return lax.ppermute(value, axis, flips)


def halve(value, axis, bit):
    halves = value.reshape(2, value.shape[0] // 2, value.shape[1])
    mine = bit_of(axis, bit)
    keep = lax.dynamic_index_in_dim(halves, mine, 0, keepdims=False)
    give = lax.dynamic_index_in_dim(halves, 1 - mine, 0, keepdims=False)
    return keep + swap(give, axis, bit)


def double(value, axis, bit):
    other = swap(value, axis, bit)
    return jnp.where(
        bit_of(axis, bit) == 0,
        jnp.concatenate([value, other]),
        jnp.concatenate([other, value]),
    )


def shift_slow(value, step, slow):
    n = slow * 2
    return lax.ppermute(value, "gy", [(i, (i + 2 * step) % n) for i in range(n)])


def sum_over_all(value):
    n_x, n_y = lax.axis_size("gx"), lax.axis_size("gy")
    bits = n_x.bit_length() - 1
    slow = n_y // 2
    mine = lax.axis_index("gy") // 2
    for bit in range(bits):
        value = halve(value, "gx", bit)
    value = halve(value, "gy", 0)
    rows, width = value.shape[0] // slow, value.shape[1]
    quarters = value.reshape(slow, rows, width)
    total = lax.dynamic_index_in_dim(quarters, mine, 0, keepdims=False)
    for step in range(1, slow):
        give = lax.dynamic_index_in_dim(quarters, (mine + step) % slow, 0, keepdims=False)
        total = total + shift_slow(give, step, slow)
    whole = jnp.zeros((slow, rows, width), value.dtype)
    whole = lax.dynamic_update_index_in_dim(whole, total, mine, 0)
    for step in range(1, slow):
        got = shift_slow(total, step, slow)
        whole = lax.dynamic_update_index_in_dim(whole, got, (mine + slow - step) % slow, 0)
    value = whole.reshape(slow * rows, width)
    value = double(value, "gy", 0)
    for bit in reversed(range(bits)):
        value = double(value, "gx", bit)
    return value


def pipelined(fields, x_factor, running_r):
    n_x, n_y = lax.axis_size("gx"), lax.axis_size("gy")
    me_x, me_y = lax.axis_index("gx"), lax.axis_index("gy")
    depth, rows, cells = fields.shape
    rank = x_factor.shape[1]
    share = rank // n_y
    cells_part = cells // n_x
    pieces = y_pieces(rows)
    by_y = jnp.transpose(fields, (1, 0, 2))

    factor = jnp.stack(
        [
            lax.dynamic_slice(x_factor, ((me_x ^ d) * depth, 0), (depth, rank)).T
            for d in range(n_x)
        ]
    )
    slow = n_y // 2
    shifts = [(dz, dy) for dz in range(slow) for dy in range(2)]

    def to(index, shift):
        return (index // 2 + shift[0]) % slow * 2 + (index % 2 + shift[1]) % 2

    def back(index, shift):
        return (index // 2 + slow - shift[0]) % slow * 2 + (index % 2 + shift[1]) % 2

    scalars = jnp.stack(
        [(me_x ^ d) * cells_part for d in range(n_x)] + [to(me_y, s) * share for s in shifts]
    ).astype(jnp.int32)
    sources = jnp.stack([back(me_y, s) for s in shifts]).astype(jnp.int32)

    chunks = [(cell, piece) for cell in range(0, cells_part, LANES) for piece in pieces]
    per_gram = len(pieces)

    flown = []

    def start(operand, axis, pairs):
        slots = range(max(0, len(flown) - 2 * WINDOW + 1), max(0, len(flown) - WINDOW + 1))
        if slots:
            operand, *passed = lax.optimization_barrier((operand, *[flown[i] for i in slots]))
            flown[slots.start : slots.stop] = passed
        flown.append(lax.ppermute(operand, axis, pairs))
        return len(flown) - 1

    def start_x(partner, send):
        return start(send, "gx", [(i, i ^ partner) for i in range(n_x)])

    def start_y(shift, send):
        return start(send, "gy", [(i, to(i, shift)) for i in range(n_y)])

    moving = []
    for index, chunk in enumerate(chunks[:AHEAD]):
        sends = pack(by_y, scalars, chunk, n_x)
        slots = []
        for (partner, _, _), send in zip(send_list(chunk, n_x), sends):
            slots.append(start_x(partner, send))
        moving.append(slots)
        if index == 0:
            near = [
                start_x(1, pack_near(by_y, scalars, cell)) for cell in range(0, cells_part, LANES)
            ]
    straight = []
    crossed = []
    carried = None

    def cross(k, j):
        pair = []
        for dz in (2 * j, 2 * j + 1):
            block = straight[k][dz]
            pair.append((flown[block] if isinstance(block, int) else block)[1])
        crossed[k][j] = start_y((0, 1), jnp.stack(pair))

    def add_gram(carried, first):
        group = range(first, first + per_gram)
        return gram(
            [[flown[b] if isinstance(b, int) else b for b in straight[k]] for k in group],
            [[flown[b] for b in crossed[k]] for k in group],
            carried,
            sources,
            pieces,
            share,
        )

    for k, chunk in enumerate(chunks):
        following = chunks[k + AHEAD] if k + AHEAD < len(chunks) else None
        after = []
        if k >= per_gram + 2 and (k - 2) % per_gram == 0:
            carried = add_gram(carried, k - 2 - per_gram)
            after.append(carried)
        outs, sends = project(
            by_y,
            flown[near[chunk[0] // LANES]],
            [flown[slot] for slot in moving[k]],
            factor,
            scalars,
            chunk,
            following,
            n_x,
            share,
            slow,
            after,
        )
        straight.append([outs[0]] + [None] * (slow - 1))
        crossed.append([None] * (slow // 2))
        steps = []
        for dz in range(1, slow):
            steps.append(((dz - 0.9) / (slow - 1), 0, dz))
        for j in range(slow // 2 if k else 0):
            steps.append(((j + 0.5) / (slow // 2), 1, j))
        slots = [None] * len(sends)
        for i in range(len(sends)):
            steps.append(((i + 0.3) / len(sends), 2, i))
        for _, kind, i in sorted(steps):
            if kind == 0:
                straight[k][i] = start_y((i, 0), outs[i])
            elif kind == 1:
                cross(k - 1, i)
            else:
                slots[i] = start_x(send_list(following, n_x)[i][0], sends[i])
        if sends:
            moving.append(slots)
    for j in range(slow // 2):
        cross(len(chunks) - 1, j)
    for first in range(0, len(chunks), per_gram):
        if first + per_gram + 2 >= len(chunks):
            carried = add_gram(carried, first)

    summed = sum_over_all(carried)
    count, size = len(pieces), pieces[0][1]
    whole = n_y * count * SUB
    blocks = {
        pair: summed[index * STEP : (index + 1) * STEP]
        for index, pair in enumerate(block_pairs(whole))
    }
    none = jnp.zeros((STEP, STEP), jnp.float32)
    starts = range(0, whole, STEP)
    upper = jnp.concatenate(
        [jnp.concatenate([blocks.get((i, j), none) for j in starts], axis=1) for i in starts]
    )
    gram_sum = upper.reshape(n_y * count, SUB, n_y * count, SUB)[:, :size, :, :size]
    return finish(gram_sum.reshape(n_y * rows, n_y * rows), running_r)


def on_device(fields, x_factor, running_r):
    n_x, n_y = lax.axis_size("gx"), lax.axis_size("gy")
    depth, rows, cells = fields.shape
    rank = x_factor.shape[1]
    fits = (
        cells % (n_x * LANES) == 0
        and rank % (2 * n_y) == 0
        and depth % 8 == 0
        and n_x & (n_x - 1) == 0
        and n_x >= 4
        and n_y % 4 == 0
        and rows >= 16
        and rows % (4 * len(y_pieces(rows))) == 0
        and n_y * pitch_of(rows) % STEP == 0
        and len(block_pairs(n_y * pitch_of(rows))) * STEP % (8 * n_x * n_y) == 0
    )
    if fits:
        return pipelined(fields, x_factor, running_r)
    return plain(fields, x_factor, running_r)


def solution(mesh):
    in_specs = (P("gx", "gy", None), P(), P())
    out_specs = P("gy", "gx")
    return jax.shard_map(
        on_device, mesh=mesh, in_specs=in_specs, out_specs=out_specs, check_vma=False
    )
```

```python
import functools

import jax
import jax.numpy as jnp
from jax import lax
from jax.experimental import pallas as pl
from jax.experimental.pallas import tpu as pltpu
from jax.sharding import PartitionSpec as P

LANES = 128
SUB = 32
STEP = 256
WINDOW = 5
AHEAD = 2
VMEM_BYTES = 56 * 1024 * 1024


def y_pieces(rows):
    count = -(-rows // SUB)
    size = rows // count
    return [(i * size, size) for i in range(count)]


def pitch_of(rows):
    return len(y_pieces(rows)) * SUB


def send_list(chunk, n_x):
    rows = chunk[1][1]
    half = rows // 2
    return [(partner, at, half) for at in (0, half) for partner in range(2, n_x)]


def copy_cells(fields, out, scalars, partner, cell, start, size, sem):
    column = pl.multiple_of(scalars[partner] + cell, LANES)
    return pltpu.make_async_copy(
        fields.at[pl.ds(start, size), :, pl.ds(column, LANES)], out, sem
    )


def chunk_copies(fields, outs, scalars, chunk, n_x, sems):
    cell, (start, _) = chunk
    return [
        copy_cells(fields, outs[i], scalars, partner, cell, start + at, size, sems.at[i])
        for i, (partner, at, size) in enumerate(send_list(chunk, n_x))
    ]


def run_pack(fields, scalars, shapes, make_copies):
    def body(scalars, fields, *rest):
        copies = make_copies(fields, rest[:-1], scalars, rest[-1])
        for copy in copies:
            copy.start()
        for copy in copies:
            copy.wait()

    return pl.pallas_call(
        body,
        out_shape=shapes,
        in_specs=[pl.BlockSpec(memory_space=pltpu.SMEM), pl.BlockSpec(memory_space=pl.ANY)],
        out_specs=[pl.BlockSpec(memory_space=pltpu.VMEM)] * len(shapes),
        scratch_shapes=[pltpu.SemaphoreType.DMA((len(shapes),))],
        compiler_params=pltpu.CompilerParams(vmem_limit_bytes=VMEM_BYTES),
        cost_estimate=pl.CostEstimate(flops=0, bytes_accessed=0, transcendentals=0),
        name="pack",
    )(scalars, fields)


def send_shapes(chunk, n_x, depth):
    return [
        jax.ShapeDtypeStruct((size, depth, LANES), jnp.bfloat16)
        for _, _, size in send_list(chunk, n_x)
    ]


def pack(fields, scalars, chunk, n_x):
    return run_pack(
        fields,
        scalars,
        send_shapes(chunk, n_x, fields.shape[1]),
        lambda fields, outs, scalars, sems: chunk_copies(fields, outs, scalars, chunk, n_x, sems),
    )


def pack_near(fields, scalars, cell):
    rows, depth = fields.shape[:2]
    return run_pack(
        fields,
        scalars,
        [jax.ShapeDtypeStruct((rows, depth, LANES), jnp.bfloat16)],
        lambda fields, outs, scalars, sems: [
            copy_cells(fields, outs[0], scalars, 1, cell, 0, rows, sems.at[0])
        ],
    )[0]


def project_kernel(chunk, following, n_x, rank, share, scalars, fields, near, got, factor, outs, sends, own, other, wide, sems):
    cell, (start, rows) = chunk
    copies = [
        copy_cells(fields, own, scalars, 0, cell, start, rows, sems.at[0]),
        pltpu.make_async_copy(near.at[pl.ds(start, rows)], other, sems.at[1]),
    ]
    for copy in copies:
        copy.start()
    packing = []
    if following is not None:
        packing = chunk_copies(
            fields, sends, scalars, following, n_x, sems.at[pl.ds(2, len(sends))]
        )
    for copy in packing:
        copy.start()
    for copy in copies:
        copy.wait()

    half = rows // 2
    many = max(n for n in range(1, 9) if half % n == 0)
    for start_row in (0, half):
        blocks = [(0, own, 0), (1, other, 0)]
        for (partner, at, _), block in zip(send_list(chunk, n_x), got):
            if at == start_row:
                blocks.append((partner, block, at))

        def one_group(group, _):
            y = start_row + group * many
            total = None
            for partner, block, at in blocks:
                right = jnp.concatenate([block[y - at + k] for k in range(many)], axis=1)
                term = jnp.dot(factor[partner], right, preferred_element_type=jnp.float32)
                total = term if total is None else total + term
            for k in range(many):
                at = pl.multiple_of((y + k) * rank, 8)
                wide[pl.ds(at, rank), :] = total[:, k * LANES : (k + 1) * LANES]
            return 0

        lax.fori_loop(0, half // many, one_group, 0)

    main = rows // 16 * 16
    left = rows - main
    halves = [out.at[i] for out in outs for i in range(out.shape[0])]
    for part, out in enumerate(halves):
        first = scalars[n_x + part]

        def one_row(i, _):
            picked = wide[pl.ds(first + i, main, stride=rank), :]
            out[pl.ds(pl.multiple_of(i * main, 16), main), :] = picked.astype(jnp.bfloat16)
            return 0

        lax.fori_loop(0, share, one_row, 0, unroll=6)
        for group in range(0, share if left else 0, 4):
            count = min(4, share - group)
            tile = [
                wide[pl.ds(main * rank + first + group + k, left, stride=rank), :]
                for k in range(count)
            ]
            tile = jnp.concatenate(tile, axis=0).astype(jnp.bfloat16)
            at = share * main + group * left
            out[at : at + count * left, :] = tile
    for copy in packing:
        copy.wait()


def project(fields, near, got, factor, scalars, chunk, following, n_x, share, slow, apart, after):
    rows = chunk[1][1]
    rank = factor.shape[1]
    depth = fields.shape[1]
    n_got = len(got)
    n_sends = 0 if following is None else n_got
    n_after = len(after)
    n_outs = 2 * slow if apart else slow
    vmem = pl.BlockSpec(memory_space=pltpu.VMEM)
    any_space = pl.BlockSpec(memory_space=pl.ANY)

    def body(scalars, fields, near, *rest):
        got = rest[:n_got]
        factor = rest[n_got]
        rest = rest[n_got + 1 + n_after :]
        outs = rest[:n_outs]
        sends = rest[n_outs : n_outs + n_sends]
        own, other, wide, sems = rest[n_outs + n_sends :]
        project_kernel(
            chunk, following, n_x, rank, share, scalars, fields, near, got, factor, outs, sends, own, other, wide, sems
        )

    shape = (1 if apart else 2, share * rows, LANES)
    shapes = [jax.ShapeDtypeStruct(shape, jnp.bfloat16)] * n_outs
    if following is not None:
        shapes += send_shapes(following, n_x, depth)
    outs = pl.pallas_call(
        body,
        out_shape=shapes,
        in_specs=[pl.BlockSpec(memory_space=pltpu.SMEM), any_space, any_space]
        + [vmem] * (n_got + 1)
        + [any_space] * n_after,
        out_specs=[vmem] * (n_outs + n_sends),
        scratch_shapes=[
            pltpu.VMEM((rows, depth, LANES), jnp.bfloat16),
            pltpu.VMEM((rows, depth, LANES), jnp.bfloat16),
            pltpu.VMEM((rows * rank, LANES), jnp.float32),
            pltpu.SemaphoreType.DMA((2 + n_got,)),
        ],
        compiler_params=pltpu.CompilerParams(vmem_limit_bytes=VMEM_BYTES),
        cost_estimate=pl.CostEstimate(flops=0, bytes_accessed=0, transcendentals=0),
        name="project",
    )(scalars, fields, near, *got, factor, *after)
    return outs[:n_outs], outs[n_outs:]


def block_pairs(whole):
    return [(i, j) for i in range(0, whole, STEP) for j in range(i, whole, STEP)]


def gram_kernel(pieces, share, places, blocks, carried, out, fibres):
    whole = fibres.shape[0]
    rows = pieces[0][1]
    main = rows // 16 * 16
    left = rows - main

    for place, block in zip(places, blocks):
        base = pl.multiple_of(place, 16)

        def one_row(i, _):
            at = pl.multiple_of(i * LANES, LANES)
            fibres[pl.ds(base, main), pl.ds(at, LANES)] = block[
                pl.ds(pl.multiple_of(i * main, 16), main), :
            ]
            return 0

        lax.fori_loop(0, share, one_row, 0, unroll=6)
        for group in range(0, share if left else 0, 4):
            count = min(4, share - group)
            at = share * main + group * left
            tile = block[at : at + count * left, :].astype(jnp.float32)
            for k in range(count):
                part = tile[k * left : (k + 1) * left, :]
                part = jnp.concatenate([part, jnp.zeros((16 - left, LANES), jnp.float32)], axis=0)
                fibres[
                    pl.ds(base + main, 16), (group + k) * LANES : (group + k + 1) * LANES
                ] = part.astype(jnp.bfloat16)

    at = 0
    for i, j in block_pairs(whole):
        product = lax.dot_general(
            fibres[i : i + STEP, :],
            fibres[j : j + STEP, :],
            (((1,), (1,)), ((), ())),
            preferred_element_type=jnp.float32,
        )
        if carried is not None:
            product = product + carried[at : at + STEP, :]
        out[at : at + STEP, :] = product
        at += STEP


def gram(arrivals, carried, sources, pieces, share):
    pitch = len(pieces) * SUB
    whole = sources.shape[0] * pitch
    entries = [(i, places) for i, piece in enumerate(arrivals) for _, places in piece]
    inputs = [block for piece in arrivals for block, _ in piece]
    size = inputs[0].shape[1]

    def body(sources, *rest):
        blocks, starts = [], []
        for ref, (i, places) in zip(rest, entries):
            for k, (dz, dy) in enumerate(places):
                blocks.append(ref.at[k])
                starts.append(sources[2 * dz + dy] * pitch + i * SUB)
        if carried is None:
            out, fibres = rest[len(inputs) :]
            before = None
        else:
            before, out, fibres = rest[len(inputs) :]
        gram_kernel(pieces, share, starts, blocks, before, out, fibres)

    specs = [
        pl.BlockSpec((len(places), size, LANES), lambda i: (0, 0, 0)) for _, places in entries
    ]
    shape = (len(block_pairs(whole)) * STEP, STEP)
    square = pl.BlockSpec(shape, lambda i: (0, 0))
    extra = [] if carried is None else [carried]
    return pl.pallas_call(
        body,
        grid=(1,),
        out_shape=jax.ShapeDtypeStruct(shape, jnp.float32),
        in_specs=[pl.BlockSpec(memory_space=pltpu.SMEM)]
        + specs
        + [square] * len(extra),
        out_specs=square,
        scratch_shapes=[pltpu.VMEM((whole, share * LANES), jnp.bfloat16)],
        compiler_params=pltpu.CompilerParams(vmem_limit_bytes=VMEM_BYTES),
        cost_estimate=pl.CostEstimate(flops=0, bytes_accessed=0, transcendentals=0),
        name="gram",
    )(sources, *inputs, *extra)


def spread_row(block, row):
    return jnp.broadcast_to(block[row : row + 1, :], block.shape)


def spread_column(block, column):
    return jnp.broadcast_to(block[:, column : column + 1], block.shape)


def factor_block(square, inverse):
    strips = len(square)
    height = square[0].shape[0]
    rows = lax.broadcasted_iota(jnp.int32, square[0].shape, 0)
    for t in range(strips):
        first = t * height
        a = square[t]
        columns = [spread_column(a, first + u) for u in range(height)]
        b = {(v, u): spread_row(columns[u], v) for u in range(height) for v in range(u + 1)}
        scale, r = [], {}
        for u in range(height):
            scale.append(lax.rsqrt(b[u, u]))
            for w in range(u + 1, height):
                r[u, w] = b[u, w] * scale[u]
            for v in range(u + 1, height):
                for w in range(v, height):
                    b[v, w] = b[v, w] - r[u, v] * r[u, w]
        inv = {}
        for v in range(height):
            for u in range(v):
                acc = r[u, v] * inv[u, u]
                for w in range(u + 1, v):
                    acc = acc + r[w, v] * inv[w, u]
                inv[v, u] = -(acc * scale[v])
            inv[v, v] = scale[v]
        new_square = new_inverse = None
        for u in range(height):
            weight = jnp.zeros_like(a)
            for v in range(u, height):
                weight = jnp.where(rows == v, inv[v, u], weight)
            one = weight * spread_row(a, u)
            two = weight * spread_row(inverse[t], u)
            new_square = one if new_square is None else new_square + one
            new_inverse = two if new_inverse is None else new_inverse + two
        square[t], inverse[t] = new_square, new_inverse
        rows_square = [spread_row(new_square, u) for u in range(height)]
        rows_inverse = [spread_row(new_inverse, u) for u in range(height)]
        for later in range(t + 1, strips):
            target = square[later]
            factors = []
            for u in range(height):
                x = spread_column(target, first + u)
                for w in range(u):
                    x = x - factors[w] * r[w, u]
                factors.append(x * scale[u])
            other = inverse[later]
            for u in range(height):
                target = target - factors[u] * rows_square[u]
                other = other - factors[u] * rows_inverse[u]
            square[later], inverse[later] = target, other


def exact_dot(left, right, contract):
    return lax.dot_general(
        left,
        right,
        (contract, ((), ())),
        precision=lax.Precision.HIGHEST,
        preferred_element_type=jnp.float32,
    )


def cholesky_kernel(slab, place, gram_sum, before, out, work):
    whole = work.shape[0]
    panels = whole // LANES
    at = 0
    for i, j in block_pairs(whole):
        work[i : i + STEP, j : j + STEP] = (
            before[i : i + STEP, j : j + STEP] + gram_sum[at : at + STEP, :]
        )
        at += STEP

    height = 8
    lane = lax.broadcasted_iota(jnp.int32, (height, LANES), 1)
    row = lax.broadcasted_iota(jnp.int32, (height, LANES), 0)

    def one_panel(p, _):
        start = pl.multiple_of(p * LANES, LANES)
        strips = LANES // height
        square, inverse = [], []
        for t in range(strips):
            square.append(work[pl.ds(start + t * height, height), pl.ds(start, LANES)])
            inverse.append(jnp.where(lane == row + t * height, 1.0, 0.0))
        factor_block(square, inverse)
        for t in range(strips):
            kept = jnp.where(lane >= row + t * height, square[t], 0.0)
            work[pl.ds(start + t * height, height), pl.ds(start, LANES)] = kept
        inverse = jnp.concatenate(inverse, axis=0)

        def one_column(j, _):
            at = pl.multiple_of(j * LANES, LANES)
            work[pl.ds(start, LANES), pl.ds(at, LANES)] = exact_dot(
                inverse, work[pl.ds(start, LANES), pl.ds(at, LANES)], ((1,), (0,))
            )
            return 0

        lax.fori_loop(p + 1, panels, one_column, 0)

        def one_row(i, _):
            row_at = pl.multiple_of(i * LANES, LANES)
            left = work[pl.ds(start, LANES), pl.ds(row_at, LANES)]

            def one_block(j, _):
                at = pl.multiple_of(j * LANES, LANES)
                term = exact_dot(left, work[pl.ds(start, LANES), pl.ds(at, LANES)], ((0,), (0,)))
                work[pl.ds(row_at, LANES), pl.ds(at, LANES)] = (
                    work[pl.ds(row_at, LANES), pl.ds(at, LANES)] - term
                )
                return 0

            lax.fori_loop(i, panels, one_block, 0)
            return 0

        lax.fori_loop(p + 1, panels, one_row, 0)
        return 0

    lax.fori_loop(0, panels, one_panel, 0)
    first = pl.multiple_of(place[0] * slab, 8)
    rows = first + lax.broadcasted_iota(jnp.int32, (slab, whole), 0)
    columns = lax.broadcasted_iota(jnp.int32, (slab, whole), 1)
    out[...] = jnp.where(columns >= rows, work[pl.ds(first, slab), :], 0.0)


def cholesky_rows(gram_sum, before, place, slab):
    whole = before.shape[0]
    vmem = pl.BlockSpec(memory_space=pltpu.VMEM)
    return pl.pallas_call(
        functools.partial(cholesky_kernel, slab),
        out_shape=jax.ShapeDtypeStruct((slab, whole), jnp.float32),
        in_specs=[pl.BlockSpec(memory_space=pltpu.SMEM), vmem, vmem],
        out_specs=vmem,
        scratch_shapes=[pltpu.VMEM((whole, whole), jnp.float32)],
        compiler_params=pltpu.CompilerParams(vmem_limit_bytes=VMEM_BYTES),
        cost_estimate=pl.CostEstimate(flops=0, bytes_accessed=0, transcendentals=0),
        name="cholesky",
    )(place, gram_sum, before)


def slice_out(upper_r):
    row_block = upper_r.shape[0] // lax.axis_size("gy")
    col_block = upper_r.shape[1] // lax.axis_size("gx")
    return lax.dynamic_slice(
        upper_r,
        (lax.axis_index("gy") * row_block, lax.axis_index("gx") * col_block),
        (row_block, col_block),
    )


def finish(gram_sum, running_r):
    total = (
        jnp.dot(
            running_r.T,
            running_r,
            precision=lax.Precision.HIGHEST,
            preferred_element_type=jnp.float32,
        )
        + gram_sum
    )
    return slice_out(lax.linalg.cholesky(total.T, symmetrize_input=False).T)


def plain(fields, x_factor, running_r):
    exchanged = lax.all_to_all(fields, "gx", split_axis=2, concat_axis=0, tiled=True)
    full_x, middle, part_cells = exchanged.shape
    product = lax.dot_general(
        x_factor,
        exchanged.reshape(full_x, middle * part_cells),
        (((0,), (0,)), ((), ())),
        preferred_element_type=jnp.float32,
    )
    projected = product.astype(jnp.bfloat16).reshape(x_factor.shape[1], middle, part_cells)
    fibres = lax.all_to_all(projected, "gy", split_axis=2, concat_axis=1, tiled=True)
    local_gram = lax.dot_general(
        fibres, fibres, (((0, 2), (0, 2)), ((), ())), preferred_element_type=jnp.float32
    )
    return finish(lax.psum(local_gram, ("gx", "gy")), running_r)


def bit_of(axis, bit):
    return (lax.axis_index(axis) >> bit) & 1


def swap(value, axis, bit):
    flips = [(i, i ^ (1 << bit)) for i in range(lax.axis_size(axis))]
    return lax.ppermute(value, axis, flips)


def halve(value, axis, bit):
    halves = value.reshape(2, value.shape[0] // 2, value.shape[1])
    mine = bit_of(axis, bit)
    keep = lax.dynamic_index_in_dim(halves, mine, 0, keepdims=False)
    give = lax.dynamic_index_in_dim(halves, 1 - mine, 0, keepdims=False)
    return keep + swap(give, axis, bit)


def double(value, axis, bit):
    other = swap(value, axis, bit)
    return jnp.where(
        bit_of(axis, bit) == 0,
        jnp.concatenate([value, other]),
        jnp.concatenate([other, value]),
    )


def shift_slow(value, step, slow):
    n = slow * 2
    return lax.ppermute(value, "gy", [(i, (i + 2 * step) % n) for i in range(n)])


def sum_over_all(value):
    n_x, n_y = lax.axis_size("gx"), lax.axis_size("gy")
    bits = n_x.bit_length() - 1
    slow = n_y // 2
    mine = lax.axis_index("gy") // 2
    for bit in range(bits):
        value = halve(value, "gx", bit)
    value = halve(value, "gy", 0)
    rows, width = value.shape[0] // slow, value.shape[1]
    quarters = value.reshape(slow, rows, width)
    total = lax.dynamic_index_in_dim(quarters, mine, 0, keepdims=False)
    for step in range(1, slow):
        give = lax.dynamic_index_in_dim(quarters, (mine + step) % slow, 0, keepdims=False)
        total = total + shift_slow(give, step, slow)
    whole = jnp.zeros((slow, rows, width), value.dtype)
    whole = lax.dynamic_update_index_in_dim(whole, total, mine, 0)
    for step in range(1, slow):
        got = shift_slow(total, step, slow)
        whole = lax.dynamic_update_index_in_dim(whole, got, (mine + slow - step) % slow, 0)
    value = whole.reshape(slow * rows, width)
    value = double(value, "gy", 0)
    for bit in reversed(range(bits)):
        value = double(value, "gx", bit)
    return value


def pipelined(fields, x_factor, running_r):
    n_x, n_y = lax.axis_size("gx"), lax.axis_size("gy")
    me_x, me_y = lax.axis_index("gx"), lax.axis_index("gy")
    depth, rows, cells = fields.shape
    rank = x_factor.shape[1]
    share = rank // n_y
    cells_part = cells // n_x
    pieces = y_pieces(rows)
    by_y = jnp.transpose(fields, (1, 0, 2))

    factor = jnp.stack(
        [
            lax.dynamic_slice(x_factor, ((me_x ^ d) * depth, 0), (depth, rank)).T
            for d in range(n_x)
        ]
    )
    slow = n_y // 2
    shifts = [(dz, dy) for dz in range(slow) for dy in range(2)]

    def to(index, shift):
        return (index // 2 + shift[0]) % slow * 2 + (index % 2 + shift[1]) % 2

    def back(index, shift):
        return (index // 2 + slow - shift[0]) % slow * 2 + (index % 2 + shift[1]) % 2

    scalars = jnp.stack(
        [(me_x ^ d) * cells_part for d in range(n_x)] + [to(me_y, s) * share for s in shifts]
    ).astype(jnp.int32)
    sources = jnp.stack([back(me_y, s) for s in shifts]).astype(jnp.int32)

    chunks = [(cell, piece) for cell in range(0, cells_part, LANES) for piece in pieces]
    per_gram = len(pieces)

    size = pieces[0][1]
    full = running_r.shape[0]
    padding = ((0, 0), (0, 0), (0, SUB - size))
    wide_r = jnp.pad(running_r.reshape(full, -1, size), padding).reshape(full, -1)
    before = exact_dot(wide_r, wide_r, ((0,), (0,)))
    padded = jnp.arange(wide_r.shape[1]) % SUB >= size
    before = before + jnp.diag(padded.astype(jnp.float32))

    flown = []

    def start(operand, axis, pairs):
        slots = range(max(0, len(flown) - 2 * WINDOW + 1), max(0, len(flown) - WINDOW + 1))
        if slots:
            operand, *passed = lax.optimization_barrier((operand, *[flown[i] for i in slots]))
            flown[slots.start : slots.stop] = passed
        flown.append(lax.ppermute(operand, axis, pairs))
        return len(flown) - 1

    def start_x(partner, send):
        return start(send, "gx", [(i, i ^ partner) for i in range(n_x)])

    def start_y(shift, send):
        return start(send, "gy", [(i, to(i, shift)) for i in range(n_y)])

    moving = []
    for index, chunk in enumerate(chunks[:AHEAD]):
        sends = pack(by_y, scalars, chunk, n_x)
        slots = []
        for (partner, _, _), send in zip(send_list(chunk, n_x), sends):
            slots.append(start_x(partner, send))
        moving.append(slots)
        if index == 0:
            near = [
                start_x(1, pack_near(by_y, scalars, cell)) for cell in range(0, cells_part, LANES)
            ]
    arrived = []
    carried = None

    def value_of(block):
        return flown[block] if isinstance(block, int) else block

    def cross(k, j):
        pair = [value_of(arrived[k][dz][0])[1] for dz in (2 * j, 2 * j + 1)]
        slot = start_y((0, 1), jnp.stack(pair))
        arrived[k].append((slot, ((2 * j, 1), (2 * j + 1, 1))))

    def add_gram(carried, first):
        group = arrived[first : first + per_gram]
        blocks = [[(value_of(block), places) for block, places in piece] for piece in group]
        return gram(blocks, carried, sources, pieces, share)

    for k, chunk in enumerate(chunks):
        following = chunks[k + AHEAD] if k + AHEAD < len(chunks) else None
        last = k == len(chunks) - 1
        after = [before] if k == 1 else []
        if k >= per_gram + 2 and (k - 2) % per_gram == 0:
            carried = add_gram(carried, k - 2 - per_gram)
            after.append(carried)
        outs, sends = project(
            by_y,
            flown[near[chunk[0] // LANES]],
            [flown[slot] for slot in moving[k]],
            factor,
            scalars,
            chunk,
            following,
            n_x,
            share,
            slow,
            last,
            after,
        )
        steps = []
        for i, place in enumerate(shifts if last else shifts[::2]):
            if i:
                steps.append(((i - 0.9) / (len(outs) - 1), 0, i))
        for j in range(slow // 2 if k else 0):
            steps.append(((j + 0.5) / (slow // 2), 1, j))
        slots = [None] * len(sends)
        for i in range(len(sends)):
            steps.append(((i + 0.3) / len(sends), 2, i))
        landed = [(outs[0], ((0, 0),))]
        arrived.append(landed)
        for _, kind, i in sorted(steps):
            if kind == 0:
                shift = shifts[i] if last else shifts[2 * i]
                landed.append((start_y(shift, outs[i]), (shift,)))
            elif kind == 1:
                cross(k - 1, i)
            else:
                slots[i] = start_x(send_list(following, n_x)[i][0], sends[i])
        if sends:
            moving.append(slots)
    for first in range(0, len(chunks), per_gram):
        if first + per_gram + 2 >= len(chunks):
            carried = add_gram(carried, first)

    summed = sum_over_all(carried)
    slab = cholesky_rows(summed, before, me_y.astype(jnp.int32)[None], pitch_of(rows))
    groups = rows * n_y // n_x // size
    mine = lax.dynamic_slice(
        slab, (0, me_x * (groups * SUB)), (slab.shape[0], groups * SUB)
    )
    mine = mine.reshape(-1, SUB, groups, SUB)[:, :size, :, :size]
    return mine.reshape(rows, groups * size)


def on_device(fields, x_factor, running_r):
    n_x, n_y = lax.axis_size("gx"), lax.axis_size("gy")
    depth, rows, cells = fields.shape
    rank = x_factor.shape[1]
    fits = (
        cells % (n_x * LANES) == 0
        and rank % (2 * n_y) == 0
        and depth % 8 == 0
        and n_x & (n_x - 1) == 0
        and n_x >= 4
        and n_y % 4 == 0
        and rows >= 16
        and rows % (4 * len(y_pieces(rows))) == 0
        and n_y * pitch_of(rows) % STEP == 0
        and rows * n_y // n_x % y_pieces(rows)[0][1] == 0
        and len(block_pairs(n_y * pitch_of(rows))) * STEP % (8 * n_x * n_y) == 0
    )
    if fits:
        return pipelined(fields, x_factor, running_r)
    return plain(fields, x_factor, running_r)


def solution(mesh):
    in_specs = (P("gx", "gy", None), P(), P())
    out_specs = P("gy", "gx")
    return jax.shard_map(
        on_device, mesh=mesh, in_specs=in_specs, out_specs=out_specs, check_vma=False
    )
```

```python
import functools

import jax
import jax.numpy as jnp
from jax import lax
from jax.experimental import pallas as pl
from jax.experimental.pallas import tpu as pltpu
from jax.sharding import PartitionSpec as P

LANES = 128
SUB = 32
STEP = 256
WINDOW = 5
AHEAD = 2
VMEM_BYTES = 56 * 1024 * 1024


def y_pieces(rows):
    count = -(-rows // SUB)
    size = rows // count
    return [(i * size, size) for i in range(count)]


def pitch_of(rows):
    return len(y_pieces(rows)) * SUB


def send_list(chunk, n_x):
    rows = chunk[1][1]
    half = rows // 2
    return [(partner, at, half) for at in (0, half) for partner in range(2, n_x)]


def copy_cells(fields, out, scalars, partner, cell, start, size, sem):
    column = pl.multiple_of(scalars[partner] + cell, LANES)
    return pltpu.make_async_copy(
        fields.at[pl.ds(start, size), :, pl.ds(column, LANES)], out, sem
    )


def chunk_copies(fields, outs, scalars, chunk, n_x, sems):
    cell, (start, _) = chunk
    return [
        copy_cells(fields, outs[i], scalars, partner, cell, start + at, size, sems.at[i])
        for i, (partner, at, size) in enumerate(send_list(chunk, n_x))
    ]


def run_pack(fields, scalars, shapes, make_copies):
    def body(scalars, fields, *rest):
        copies = make_copies(fields, rest[:-1], scalars, rest[-1])
        for copy in copies:
            copy.start()
        for copy in copies:
            copy.wait()

    return pl.pallas_call(
        body,
        out_shape=shapes,
        in_specs=[pl.BlockSpec(memory_space=pltpu.SMEM), pl.BlockSpec(memory_space=pl.ANY)],
        out_specs=[pl.BlockSpec(memory_space=pltpu.VMEM)] * len(shapes),
        scratch_shapes=[pltpu.SemaphoreType.DMA((len(shapes),))],
        compiler_params=pltpu.CompilerParams(vmem_limit_bytes=VMEM_BYTES),
        cost_estimate=pl.CostEstimate(flops=0, bytes_accessed=0, transcendentals=0),
        name="pack",
    )(scalars, fields)


def send_shapes(chunk, n_x, depth):
    return [
        jax.ShapeDtypeStruct((size, depth, LANES), jnp.bfloat16)
        for _, _, size in send_list(chunk, n_x)
    ]


def pack(fields, scalars, chunk, n_x):
    return run_pack(
        fields,
        scalars,
        send_shapes(chunk, n_x, fields.shape[1]),
        lambda fields, outs, scalars, sems: chunk_copies(fields, outs, scalars, chunk, n_x, sems),
    )


def pack_near(fields, scalars, cell):
    rows, depth = fields.shape[:2]
    return run_pack(
        fields,
        scalars,
        [jax.ShapeDtypeStruct((rows, depth, LANES), jnp.bfloat16)],
        lambda fields, outs, scalars, sems: [
            copy_cells(fields, outs[0], scalars, 1, cell, 0, rows, sems.at[0])
        ],
    )[0]


def project_kernel(chunk, following, n_x, rank, share, scalars, fields, near, got, factor, outs, sends, own, other, wide, sems):
    cell, (start, rows) = chunk
    copies = [
        copy_cells(fields, own, scalars, 0, cell, start, rows, sems.at[0]),
        pltpu.make_async_copy(near.at[pl.ds(start, rows)], other, sems.at[1]),
    ]
    for copy in copies:
        copy.start()
    packing = []
    if following is not None:
        packing = chunk_copies(
            fields, sends, scalars, following, n_x, sems.at[pl.ds(2, len(sends))]
        )
    for copy in packing:
        copy.start()
    for copy in copies:
        copy.wait()

    half = rows // 2
    many = max(n for n in range(1, 9) if half % n == 0)
    for start_row in (0, half):
        blocks = [(0, own, 0), (1, other, 0)]
        for (partner, at, _), block in zip(send_list(chunk, n_x), got):
            if at == start_row:
                blocks.append((partner, block, at))

        def one_group(group, _):
            y = start_row + group * many
            total = None
            for partner, block, at in blocks:
                right = jnp.concatenate([block[y - at + k] for k in range(many)], axis=1)
                term = jnp.dot(factor[partner], right, preferred_element_type=jnp.float32)
                total = term if total is None else total + term
            for k in range(many):
                at = pl.multiple_of((y + k) * rank, 8)
                wide[pl.ds(at, rank), :] = total[:, k * LANES : (k + 1) * LANES]
            return 0

        lax.fori_loop(0, half // many, one_group, 0)

    main = rows // 16 * 16
    left = rows - main
    halves = [out.at[i] for out in outs for i in range(out.shape[0])]
    groups = halves[0].shape[0]
    per = share // groups
    for part, at_group in [(p, g) for p in range(len(halves)) for g in range(groups)]:
        out = halves[part].at[at_group]
        first = scalars[n_x + part] + at_group * per

        def one_row(i, _):
            picked = wide[pl.ds(first + i, main, stride=rank), :]
            out[pl.ds(pl.multiple_of(i * main, 16), main), :] = picked.astype(jnp.bfloat16)
            return 0

        lax.fori_loop(0, per, one_row, 0, unroll=7)
        for four in range(0, per if left else 0, 4):
            count = min(4, per - four)
            tile = [
                wide[pl.ds(main * rank + first + four + k, left, stride=rank), :]
                for k in range(count)
            ]
            tile = jnp.concatenate(tile, axis=0).astype(jnp.bfloat16)
            at = per * main + four * left
            out[at : at + count * left, :] = tile
    for copy in packing:
        copy.wait()


def project(fields, near, got, factor, scalars, chunk, following, n_x, share, slow, apart, after):
    rows = chunk[1][1]
    rank = factor.shape[1]
    depth = fields.shape[1]
    n_got = len(got)
    n_sends = 0 if following is None else n_got
    n_after = len(after)
    n_outs = 2 * slow if apart else slow
    vmem = pl.BlockSpec(memory_space=pltpu.VMEM)
    any_space = pl.BlockSpec(memory_space=pl.ANY)

    def body(scalars, fields, near, *rest):
        got = rest[:n_got]
        factor = rest[n_got]
        rest = rest[n_got + 1 + n_after :]
        outs = rest[:n_outs]
        sends = rest[n_outs : n_outs + n_sends]
        own, other, wide, sems = rest[n_outs + n_sends :]
        project_kernel(
            chunk, following, n_x, rank, share, scalars, fields, near, got, factor, outs, sends, own, other, wide, sems
        )

    groups = column_groups(share)
    shape = (1 if apart else 2, groups, share // groups * rows, LANES)
    shapes = [jax.ShapeDtypeStruct(shape, jnp.bfloat16)] * n_outs
    if following is not None:
        shapes += send_shapes(following, n_x, depth)
    outs = pl.pallas_call(
        body,
        out_shape=shapes,
        in_specs=[pl.BlockSpec(memory_space=pltpu.SMEM), any_space, any_space]
        + [vmem] * (n_got + 1)
        + [any_space] * n_after,
        out_specs=[vmem] * (n_outs + n_sends),
        scratch_shapes=[
            pltpu.VMEM((rows, depth, LANES), jnp.bfloat16),
            pltpu.VMEM((rows, depth, LANES), jnp.bfloat16),
            pltpu.VMEM((rows * rank, LANES), jnp.float32),
            pltpu.SemaphoreType.DMA((2 + n_got,)),
        ],
        compiler_params=pltpu.CompilerParams(vmem_limit_bytes=VMEM_BYTES),
        cost_estimate=pl.CostEstimate(flops=0, bytes_accessed=0, transcendentals=0),
        name="project",
    )(scalars, fields, near, *got, factor, *after)
    return outs[:n_outs], outs[n_outs:]


def column_groups(share):
    return 3 if share % 6 == 0 else 1


def block_pairs(whole):
    return [(i, j) for i in range(0, whole, STEP) for j in range(i, whole, STEP)]


def gram_kernel(pieces, per, places, blocks, carried, out, fibres):
    whole = fibres.shape[0]
    rows = pieces[0][1]
    main = rows // 16 * 16
    left = rows - main

    @pl.when(pl.program_id(0) == 0)
    def _():
        out[...] = jnp.zeros_like(out) if carried is None else carried[...]

    for place, block in zip(places, blocks):
        base = pl.multiple_of(place, 16)

        def one_row(i, _):
            at = pl.multiple_of(i * LANES, LANES)
            fibres[pl.ds(base, main), pl.ds(at, LANES)] = block[
                pl.ds(pl.multiple_of(i * main, 16), main), :
            ]
            return 0

        lax.fori_loop(0, per, one_row, 0, unroll=7)
        for group in range(0, per if left else 0, 4):
            count = min(4, per - group)
            at = per * main + group * left
            tile = block[at : at + count * left, :].astype(jnp.float32)
            for k in range(count):
                part = tile[k * left : (k + 1) * left, :]
                part = jnp.concatenate([part, jnp.zeros((16 - left, LANES), jnp.float32)], axis=0)
                fibres[
                    pl.ds(base + main, 16), (group + k) * LANES : (group + k + 1) * LANES
                ] = part.astype(jnp.bfloat16)

    at = 0
    for i in range(0, whole, STEP):
        product = lax.dot_general(
            fibres[i : i + STEP, :],
            fibres[i:, :],
            (((1,), (1,)), ((), ())),
            preferred_element_type=jnp.float32,
        )
        for j in range(0, whole - i, STEP):
            out[at : at + STEP, :] = out[at : at + STEP, :] + product[:, j : j + STEP]
            at += STEP


def gram(arrivals, carried, sources, pieces, share):
    pitch = len(pieces) * SUB
    whole = sources.shape[0] * pitch
    entries = [(i, places) for i, piece in enumerate(arrivals) for _, places in piece]
    inputs = [block for piece in arrivals for block, _ in piece]
    groups, size = inputs[0].shape[1:3]

    def body(sources, *rest):
        blocks, starts = [], []
        for ref, (i, places) in zip(rest, entries):
            for k, (dz, dy) in enumerate(places):
                blocks.append(ref.at[k, 0])
                starts.append(sources[2 * dz + dy] * pitch + i * SUB)
        if carried is None:
            out, fibres = rest[len(inputs) :]
            before = None
        else:
            before, out, fibres = rest[len(inputs) :]
        gram_kernel(pieces, share // groups, starts, blocks, before, out, fibres)

    specs = [
        pl.BlockSpec((len(places), 1, size, LANES), lambda g: (0, g, 0, 0)) for _, places in entries
    ]
    shape = (len(block_pairs(whole)) * STEP, STEP)
    square = pl.BlockSpec(shape, lambda g: (0, 0))
    extra = [] if carried is None else [carried]
    return pl.pallas_call(
        body,
        grid=(groups,),
        out_shape=jax.ShapeDtypeStruct(shape, jnp.float32),
        in_specs=[pl.BlockSpec(memory_space=pltpu.SMEM)]
        + specs
        + [square] * len(extra),
        out_specs=square,
        scratch_shapes=[pltpu.VMEM((whole, share // groups * LANES), jnp.bfloat16)],
        compiler_params=pltpu.CompilerParams(vmem_limit_bytes=VMEM_BYTES),
        cost_estimate=pl.CostEstimate(flops=0, bytes_accessed=0, transcendentals=0),
        name="gram",
    )(sources, *inputs, *extra)


def spread_row(block, row):
    return jnp.broadcast_to(block[row : row + 1, :], block.shape)


def spread_column(block, column):
    return jnp.broadcast_to(block[:, column : column + 1], block.shape)


def factor_block(square, inverse):
    strips = len(square)
    height = square[0].shape[0]
    rows = lax.broadcasted_iota(jnp.int32, square[0].shape, 0)
    for t in range(strips):
        first = t * height
        a = square[t]
        columns = [spread_column(a, first + u) for u in range(height)]
        b = {(v, u): spread_row(columns[u], v) for u in range(height) for v in range(u + 1)}
        scale, r = [], {}
        for u in range(height):
            scale.append(lax.rsqrt(b[u, u]))
            for w in range(u + 1, height):
                r[u, w] = b[u, w] * scale[u]
            for v in range(u + 1, height):
                for w in range(v, height):
                    b[v, w] = b[v, w] - r[u, v] * r[u, w]
        inv = {}
        for v in range(height):
            for u in range(v):
                acc = r[u, v] * inv[u, u]
                for w in range(u + 1, v):
                    acc = acc + r[w, v] * inv[w, u]
                inv[v, u] = -(acc * scale[v])
            inv[v, v] = scale[v]
        new_square = new_inverse = None
        for u in range(height):
            weight = jnp.zeros_like(a)
            for v in range(u, height):
                weight = jnp.where(rows == v, inv[v, u], weight)
            one = weight * spread_row(a, u)
            two = weight * spread_row(inverse[t], u)
            new_square = one if new_square is None else new_square + one
            new_inverse = two if new_inverse is None else new_inverse + two
        square[t], inverse[t] = new_square, new_inverse
        rows_square = [spread_row(new_square, u) for u in range(height)]
        rows_inverse = [spread_row(new_inverse, u) for u in range(height)]
        for later in range(t + 1, strips):
            target = square[later]
            factors = []
            for u in range(height):
                x = spread_column(target, first + u)
                for w in range(u):
                    x = x - factors[w] * r[w, u]
                factors.append(x * scale[u])
            other = inverse[later]
            for u in range(height):
                target = target - factors[u] * rows_square[u]
                other = other - factors[u] * rows_inverse[u]
            square[later], inverse[later] = target, other


def exact_dot(left, right, contract):
    return lax.dot_general(
        left,
        right,
        (contract, ((), ())),
        precision=lax.Precision.HIGHEST,
        preferred_element_type=jnp.float32,
    )


def cholesky_kernel(slab, place, gram_sum, before, out, work):
    whole = work.shape[0]
    panels = whole // LANES
    at = 0
    for i, j in block_pairs(whole):
        work[i : i + STEP, j : j + STEP] = (
            before[i : i + STEP, j : j + STEP] + gram_sum[at : at + STEP, :]
        )
        at += STEP

    height = 8
    lane = lax.broadcasted_iota(jnp.int32, (height, LANES), 1)
    row = lax.broadcasted_iota(jnp.int32, (height, LANES), 0)

    def one_panel(p, _):
        start = pl.multiple_of(p * LANES, LANES)
        strips = LANES // height
        square, inverse = [], []
        for t in range(strips):
            square.append(work[pl.ds(start + t * height, height), pl.ds(start, LANES)])
            inverse.append(jnp.where(lane == row + t * height, 1.0, 0.0))
        factor_block(square, inverse)
        for t in range(strips):
            kept = jnp.where(lane >= row + t * height, square[t], 0.0)
            work[pl.ds(start + t * height, height), pl.ds(start, LANES)] = kept
        inverse = jnp.concatenate(inverse, axis=0)

        def one_column(j, _):
            at = pl.multiple_of(j * LANES, LANES)
            work[pl.ds(start, LANES), pl.ds(at, LANES)] = exact_dot(
                inverse, work[pl.ds(start, LANES), pl.ds(at, LANES)], ((1,), (0,))
            )
            return 0

        lax.fori_loop(p + 1, panels, one_column, 0)

        def one_row(i, _):
            row_at = pl.multiple_of(i * LANES, LANES)
            left = work[pl.ds(start, LANES), pl.ds(row_at, LANES)]

            def one_block(j, _):
                at = pl.multiple_of(j * LANES, LANES)
                term = exact_dot(left, work[pl.ds(start, LANES), pl.ds(at, LANES)], ((0,), (0,)))
                work[pl.ds(row_at, LANES), pl.ds(at, LANES)] = (
                    work[pl.ds(row_at, LANES), pl.ds(at, LANES)] - term
                )
                return 0

            lax.fori_loop(i, panels, one_block, 0)
            return 0

        lax.fori_loop(p + 1, panels, one_row, 0)
        return 0

    lax.fori_loop(0, panels, one_panel, 0)
    first = pl.multiple_of(place[0] * slab, 8)
    rows = first + lax.broadcasted_iota(jnp.int32, (slab, whole), 0)
    columns = lax.broadcasted_iota(jnp.int32, (slab, whole), 1)
    out[...] = jnp.where(columns >= rows, work[pl.ds(first, slab), :], 0.0)


def cholesky_rows(gram_sum, before, place, slab):
    whole = before.shape[0]
    vmem = pl.BlockSpec(memory_space=pltpu.VMEM)
    return pl.pallas_call(
        functools.partial(cholesky_kernel, slab),
        out_shape=jax.ShapeDtypeStruct((slab, whole), jnp.float32),
        in_specs=[pl.BlockSpec(memory_space=pltpu.SMEM), vmem, vmem],
        out_specs=vmem,
        scratch_shapes=[pltpu.VMEM((whole, whole), jnp.float32)],
        compiler_params=pltpu.CompilerParams(vmem_limit_bytes=VMEM_BYTES),
        cost_estimate=pl.CostEstimate(flops=0, bytes_accessed=0, transcendentals=0),
        name="cholesky",
    )(place, gram_sum, before)


def slice_out(upper_r):
    row_block = upper_r.shape[0] // lax.axis_size("gy")
    col_block = upper_r.shape[1] // lax.axis_size("gx")
    return lax.dynamic_slice(
        upper_r,
        (lax.axis_index("gy") * row_block, lax.axis_index("gx") * col_block),
        (row_block, col_block),
    )


def finish(gram_sum, running_r):
    total = (
        jnp.dot(
            running_r.T,
            running_r,
            precision=lax.Precision.HIGHEST,
            preferred_element_type=jnp.float32,
        )
        + gram_sum
    )
    return slice_out(lax.linalg.cholesky(total.T, symmetrize_input=False).T)


def plain(fields, x_factor, running_r):
    exchanged = lax.all_to_all(fields, "gx", split_axis=2, concat_axis=0, tiled=True)
    full_x, middle, part_cells = exchanged.shape
    product = lax.dot_general(
        x_factor,
        exchanged.reshape(full_x, middle * part_cells),
        (((0,), (0,)), ((), ())),
        preferred_element_type=jnp.float32,
    )
    projected = product.astype(jnp.bfloat16).reshape(x_factor.shape[1], middle, part_cells)
    fibres = lax.all_to_all(projected, "gy", split_axis=2, concat_axis=1, tiled=True)
    local_gram = lax.dot_general(
        fibres, fibres, (((0, 2), (0, 2)), ((), ())), preferred_element_type=jnp.float32
    )
    return finish(lax.psum(local_gram, ("gx", "gy")), running_r)


def bit_of(axis, bit):
    return (lax.axis_index(axis) >> bit) & 1


def swap(value, axis, bit):
    flips = [(i, i ^ (1 << bit)) for i in range(lax.axis_size(axis))]
    return lax.ppermute(value, axis, flips)


def halve(value, axis, bit):
    halves = value.reshape(2, value.shape[0] // 2, value.shape[1])
    mine = bit_of(axis, bit)
    keep = lax.dynamic_index_in_dim(halves, mine, 0, keepdims=False)
    give = lax.dynamic_index_in_dim(halves, 1 - mine, 0, keepdims=False)
    return keep + swap(give, axis, bit)


def double(value, axis, bit):
    other = swap(value, axis, bit)
    return jnp.where(
        bit_of(axis, bit) == 0,
        jnp.concatenate([value, other]),
        jnp.concatenate([other, value]),
    )


def shift_slow(value, step, slow):
    n = slow * 2
    return lax.ppermute(value, "gy", [(i, (i + 2 * step) % n) for i in range(n)])


def sum_over_all(value):
    n_x, n_y = lax.axis_size("gx"), lax.axis_size("gy")
    bits = n_x.bit_length() - 1
    slow = n_y // 2
    mine = lax.axis_index("gy") // 2
    for bit in range(bits):
        value = halve(value, "gx", bit)
    value = halve(value, "gy", 0)
    rows, width = value.shape[0] // slow, value.shape[1]
    quarters = value.reshape(slow, rows, width)
    total = lax.dynamic_index_in_dim(quarters, mine, 0, keepdims=False)
    for step in range(1, slow):
        give = lax.dynamic_index_in_dim(quarters, (mine + step) % slow, 0, keepdims=False)
        total = total + shift_slow(give, step, slow)
    whole = jnp.zeros((slow, rows, width), value.dtype)
    whole = lax.dynamic_update_index_in_dim(whole, total, mine, 0)
    for step in range(1, slow):
        got = shift_slow(total, step, slow)
        whole = lax.dynamic_update_index_in_dim(whole, got, (mine + slow - step) % slow, 0)
    value = whole.reshape(slow * rows, width)
    value = double(value, "gy", 0)
    for bit in reversed(range(bits)):
        value = double(value, "gx", bit)
    return value


def pipelined(fields, x_factor, running_r):
    n_x, n_y = lax.axis_size("gx"), lax.axis_size("gy")
    me_x, me_y = lax.axis_index("gx"), lax.axis_index("gy")
    depth, rows, cells = fields.shape
    rank = x_factor.shape[1]
    share = rank // n_y
    cells_part = cells // n_x
    pieces = y_pieces(rows)
    by_y = jnp.transpose(fields, (1, 0, 2))

    factor = jnp.stack(
        [
            lax.dynamic_slice(x_factor, ((me_x ^ d) * depth, 0), (depth, rank)).T
            for d in range(n_x)
        ]
    )
    slow = n_y // 2
    shifts = [(dz, dy) for dz in range(slow) for dy in range(2)]

    def to(index, shift):
        return (index // 2 + shift[0]) % slow * 2 + (index % 2 + shift[1]) % 2

    def back(index, shift):
        return (index // 2 + slow - shift[0]) % slow * 2 + (index % 2 + shift[1]) % 2

    scalars = jnp.stack(
        [(me_x ^ d) * cells_part for d in range(n_x)] + [to(me_y, s) * share for s in shifts]
    ).astype(jnp.int32)
    sources = jnp.stack([back(me_y, s) for s in shifts]).astype(jnp.int32)

    chunks = [(cell, piece) for cell in range(0, cells_part, LANES) for piece in pieces]
    per_gram = len(pieces)

    size = pieces[0][1]
    full = running_r.shape[0]
    padding = ((0, 0), (0, 0), (0, SUB - size))
    wide_r = jnp.pad(running_r.reshape(full, -1, size), padding).reshape(full, -1)
    before = exact_dot(wide_r, wide_r, ((0,), (0,)))
    padded = jnp.arange(wide_r.shape[1]) % SUB >= size
    before = before + jnp.diag(padded.astype(jnp.float32))

    flown = []

    def start(operand, axis, pairs):
        slots = range(max(0, len(flown) - 2 * WINDOW + 1), max(0, len(flown) - WINDOW + 1))
        if slots:
            operand, *passed = lax.optimization_barrier((operand, *[flown[i] for i in slots]))
            flown[slots.start : slots.stop] = passed
        flown.append(lax.ppermute(operand, axis, pairs))
        return len(flown) - 1

    def start_x(partner, send):
        return start(send, "gx", [(i, i ^ partner) for i in range(n_x)])

    def start_y(shift, send):
        return start(send, "gy", [(i, to(i, shift)) for i in range(n_y)])

    moving = []
    for index, chunk in enumerate(chunks[:AHEAD]):
        sends = pack(by_y, scalars, chunk, n_x)
        slots = []
        for (partner, _, _), send in zip(send_list(chunk, n_x), sends):
            slots.append(start_x(partner, send))
        moving.append(slots)
        if index == 0:
            near = [
                start_x(1, pack_near(by_y, scalars, cell)) for cell in range(0, cells_part, LANES)
            ]
    arrived = []
    carried = None

    def value_of(block):
        return flown[block] if isinstance(block, int) else block

    def cross(k, j):
        pair = [value_of(arrived[k][dz][0])[1] for dz in (2 * j, 2 * j + 1)]
        slot = start_y((0, 1), jnp.stack(pair))
        arrived[k].append((slot, ((2 * j, 1), (2 * j + 1, 1))))

    def add_gram(carried, first):
        group = arrived[first : first + per_gram]
        blocks = [[(value_of(block), places) for block, places in piece] for piece in group]
        return gram(blocks, carried, sources, pieces, share)

    for k, chunk in enumerate(chunks):
        following = chunks[k + AHEAD] if k + AHEAD < len(chunks) else None
        last = k == len(chunks) - 1
        after = [before] if k == 1 else []
        if k >= per_gram + 2 and (k - 2) % per_gram == 0:
            carried = add_gram(carried, k - 2 - per_gram)
            after.append(carried)
        outs, sends = project(
            by_y,
            flown[near[chunk[0] // LANES]],
            [flown[slot] for slot in moving[k]],
            factor,
            scalars,
            chunk,
            following,
            n_x,
            share,
            slow,
            last,
            after,
        )
        steps = []
        for i, place in enumerate(shifts if last else shifts[::2]):
            if i:
                steps.append((((i if last else [1, 3, 2][i - 1]) - (3.5 if k == 0 else 0.9)) / (len(outs) - 1), 0, i))
        for j in range(slow // 2 if k else 0):
            steps.append(((j + 0.5) / (slow // 2), 1, j))
        slots = [None] * len(sends)
        for i in range(len(sends)):
            steps.append(((i + 1.2) / len(sends), 2, i))
        landed = [(outs[0], ((0, 0),))] + [None] * (len(outs) - 1)
        arrived.append(landed)
        for _, kind, i in sorted(steps):
            if kind == 0:
                shift = shifts[i] if last else shifts[2 * i]
                landed[i] = (start_y(shift, outs[i]), (shift,))
            elif kind == 1:
                cross(k - 1, i)
            else:
                slots[i] = start_x(send_list(following, n_x)[i][0], sends[i])
        if sends:
            moving.append(slots)
    for first in range(0, len(chunks), per_gram):
        if first + per_gram + 2 >= len(chunks):
            carried = add_gram(carried, first)

    summed = sum_over_all(carried)
    slab = cholesky_rows(summed, before, me_y.astype(jnp.int32)[None], pitch_of(rows))
    groups = rows * n_y // n_x // size
    mine = lax.dynamic_slice(
        slab, (0, me_x * (groups * SUB)), (slab.shape[0], groups * SUB)
    )
    mine = mine.reshape(-1, SUB, groups, SUB)[:, :size, :, :size]
    return mine.reshape(rows, groups * size)


def on_device(fields, x_factor, running_r):
    n_x, n_y = lax.axis_size("gx"), lax.axis_size("gy")
    depth, rows, cells = fields.shape
    rank = x_factor.shape[1]
    fits = (
        cells % (n_x * LANES) == 0
        and rank % (2 * n_y) == 0
        and depth % 8 == 0
        and n_x & (n_x - 1) == 0
        and n_x >= 4
        and n_y % 4 == 0
        and rows >= 16
        and rows % (4 * len(y_pieces(rows))) == 0
        and n_y * pitch_of(rows) % STEP == 0
        and rows * n_y // n_x % y_pieces(rows)[0][1] == 0
        and len(block_pairs(n_y * pitch_of(rows))) * STEP % (8 * n_x * n_y) == 0
    )
    if fits:
        return pipelined(fields, x_factor, running_r)
    return plain(fields, x_factor, running_r)


def solution(mesh):
    in_specs = (P("gx", "gy", None), P(), P())
    out_specs = P("gy", "gx")
    return jax.shard_map(
        on_device, mesh=mesh, in_specs=in_specs, out_specs=out_specs, check_vma=False
    )
```

```python
import functools

import jax
import jax.numpy as jnp
from jax import lax
from jax.experimental import pallas as pl
from jax.experimental.pallas import tpu as pltpu
from jax.sharding import PartitionSpec as P

LANES = 128
SUB = 32
STEP = 256
WINDOW = 5
AHEAD = 2
VMEM_BYTES = 56 * 1024 * 1024


def y_pieces(rows):
    count = -(-rows // SUB)
    size = rows // count
    return [(i * size, size) for i in range(count)]


def pitch_of(rows):
    return len(y_pieces(rows)) * SUB


def send_list(chunk, n_x):
    rows = chunk[1][1]
    half = rows // 2
    return [(partner, at, half) for at in (0, half) for partner in range(2, n_x)]


def copy_cells(fields, out, scalars, partner, cell, start, size, sem):
    column = pl.multiple_of(scalars[partner] + cell, LANES)
    return pltpu.make_async_copy(
        fields.at[pl.ds(start, size), :, pl.ds(column, LANES)], out, sem
    )


def chunk_copies(fields, outs, scalars, chunk, n_x, sems):
    cell, (start, _) = chunk
    return [
        copy_cells(fields, outs[i], scalars, partner, cell, start + at, size, sems.at[i])
        for i, (partner, at, size) in enumerate(send_list(chunk, n_x))
    ]


def run_pack(fields, scalars, shapes, make_copies, after=()):
    def body(scalars, fields, *rest):
        rest = rest[len(after) :]
        copies = make_copies(fields, rest[:-1], scalars, rest[-1])
        for copy in copies:
            copy.start()
        for copy in copies:
            copy.wait()

    return pl.pallas_call(
        body,
        out_shape=shapes,
        in_specs=[pl.BlockSpec(memory_space=pltpu.SMEM)]
        + [pl.BlockSpec(memory_space=pl.ANY)] * (1 + len(after)),
        out_specs=[pl.BlockSpec(memory_space=pltpu.VMEM)] * len(shapes),
        scratch_shapes=[pltpu.SemaphoreType.DMA((len(shapes),))],
        compiler_params=pltpu.CompilerParams(vmem_limit_bytes=VMEM_BYTES),
        cost_estimate=pl.CostEstimate(flops=0, bytes_accessed=0, transcendentals=0),
        name="pack",
    )(scalars, fields, *after)


def send_shapes(chunk, n_x, depth):
    return [
        jax.ShapeDtypeStruct((size, depth, LANES), jnp.bfloat16)
        for _, _, size in send_list(chunk, n_x)
    ]


def pack(fields, scalars, chunk, n_x, after):
    return run_pack(
        fields,
        scalars,
        send_shapes(chunk, n_x, fields.shape[1]),
        lambda fields, outs, scalars, sems: chunk_copies(fields, outs, scalars, chunk, n_x, sems),
        after,
    )


def pack_near(fields, scalars, cell):
    rows, depth = fields.shape[:2]
    return run_pack(
        fields,
        scalars,
        [jax.ShapeDtypeStruct((rows, depth, LANES), jnp.bfloat16)],
        lambda fields, outs, scalars, sems: [
            copy_cells(fields, outs[0], scalars, 1, cell, 0, rows, sems.at[0])
        ],
    )[0]


def project_kernel(chunk, following, n_x, rank, share, scalars, fields, near, got, factor, outs, sends, own, other, wide, held, sems, out_sems):
    cell, (start, rows) = chunk
    copies = [
        copy_cells(fields, own, scalars, 0, cell, start, rows, sems.at[0]),
        pltpu.make_async_copy(near.at[pl.ds(start, rows)], other, sems.at[1]),
    ]
    for copy in copies:
        copy.start()
    packing = []
    if following is not None:
        packing = chunk_copies(
            fields, held, scalars, following, n_x, sems.at[pl.ds(2, len(sends))]
        )
    for copy in packing:
        copy.start()
    for copy in copies:
        copy.wait()

    leaving = []
    half = rows // 2
    many = max(n for n in range(1, 9) if half % n == 0)
    for start_row in (0, half):
        blocks = [(0, own, 0), (1, other, 0)]
        for (partner, at, _), block in zip(send_list(chunk, n_x), got):
            if at == start_row:
                blocks.append((partner, block, at))

        def one_group(group, _):
            y = start_row + group * many
            total = None
            for partner, block, at in blocks:
                right = jnp.concatenate([block[y - at + k] for k in range(many)], axis=1)
                term = jnp.dot(factor[partner], right, preferred_element_type=jnp.float32)
                total = term if total is None else total + term
            for k in range(many):
                at = pl.multiple_of((y + k) * rank, 8)
                wide[pl.ds(at, rank), :] = total[:, k * LANES : (k + 1) * LANES]
            return 0

        lax.fori_loop(0, half // many, one_group, 0)
        if start_row == 0:
            for i, copy in enumerate(packing):
                copy.wait()
                leaving.append(pltpu.make_async_copy(held[i], sends[i], out_sems.at[i]))
                leaving[i].start()

    main = rows // 16 * 16
    left = rows - main
    halves = [out.at[i] for out in outs for i in range(out.shape[0])]
    groups = halves[0].shape[0]
    per = share // groups
    for part, at_group in [(p, g) for p in range(len(halves)) for g in range(groups)]:
        out = halves[part].at[at_group]
        first = scalars[n_x + part] + at_group * per

        def one_row(i, _):
            picked = wide[pl.ds(first + i, main, stride=rank), :]
            out[pl.ds(pl.multiple_of(i * main, 16), main), :] = picked.astype(jnp.bfloat16)
            return 0

        lax.fori_loop(0, per, one_row, 0, unroll=7)
        for four in range(0, per if left else 0, 4):
            count = min(4, per - four)
            tile = [
                wide[pl.ds(main * rank + first + four + k, left, stride=rank), :]
                for k in range(count)
            ]
            tile = jnp.concatenate(tile, axis=0).astype(jnp.bfloat16)
            at = per * main + four * left
            out[at : at + count * left, :] = tile
    for copy in leaving:
        copy.wait()


def project(fields, near, got, factor, scalars, chunk, following, n_x, share, slow, apart, after):
    rows = chunk[1][1]
    rank = factor.shape[1]
    depth = fields.shape[1]
    n_got = len(got)
    n_sends = 0 if following is None else n_got
    n_after = len(after)
    n_outs = 2 * slow if apart else slow
    vmem = pl.BlockSpec(memory_space=pltpu.VMEM)
    any_space = pl.BlockSpec(memory_space=pl.ANY)

    def body(scalars, fields, near, *rest):
        got = rest[:n_got]
        factor = rest[n_got]
        rest = rest[n_got + 1 + n_after :]
        outs = rest[:n_outs]
        sends = rest[n_outs : n_outs + n_sends]
        own, other, wide, sems, out_sems = rest[n_outs + n_sends : n_outs + n_sends + 5]
        held = rest[n_outs + n_sends + 5 :]
        project_kernel(
            chunk, following, n_x, rank, share, scalars, fields, near, got, factor, outs, sends, own, other, wide, held, sems, out_sems
        )

    groups = column_groups(share)
    shape = (1 if apart else 2, groups, share // groups * rows, LANES)
    shapes = [jax.ShapeDtypeStruct(shape, jnp.bfloat16)] * n_outs
    if following is not None:
        shapes += send_shapes(following, n_x, depth)
    outs = pl.pallas_call(
        body,
        out_shape=shapes,
        in_specs=[pl.BlockSpec(memory_space=pltpu.SMEM), any_space, any_space]
        + [vmem] * (n_got + 1)
        + [any_space] * n_after,
        out_specs=[vmem] * n_outs + [any_space] * n_sends,
        scratch_shapes=[
            pltpu.VMEM((rows, depth, LANES), jnp.bfloat16),
            pltpu.VMEM((rows, depth, LANES), jnp.bfloat16),
            pltpu.VMEM((rows * rank, LANES), jnp.float32),
            pltpu.SemaphoreType.DMA((2 + n_got,)),
            pltpu.SemaphoreType.DMA((n_got,)),
        ]
        + [pltpu.VMEM(shape.shape, shape.dtype) for shape in shapes[n_outs:]],
        compiler_params=pltpu.CompilerParams(vmem_limit_bytes=VMEM_BYTES),
        cost_estimate=pl.CostEstimate(flops=0, bytes_accessed=0, transcendentals=0),
        name="project",
    )(scalars, fields, near, *got, factor, *after)
    return outs[:n_outs], outs[n_outs:]


def column_groups(share):
    return 3 if share % 6 == 0 else 1


def block_pairs(whole):
    return [(i, j) for i in range(0, whole, STEP) for j in range(i, whole, STEP)]


def gram_kernel(pieces, per, places, blocks, carried, out, fibres):
    whole = fibres.shape[0]
    rows = pieces[0][1]
    main = rows // 16 * 16
    left = rows - main

    @pl.when(pl.program_id(0) == 0)
    def _():
        out[...] = jnp.zeros_like(out) if carried is None else carried[...]

    for place, block in zip(places, blocks):
        base = pl.multiple_of(place, 16)

        def one_row(i, _):
            at = pl.multiple_of(i * LANES, LANES)
            fibres[pl.ds(base, main), pl.ds(at, LANES)] = block[
                pl.ds(pl.multiple_of(i * main, 16), main), :
            ]
            return 0

        lax.fori_loop(0, per, one_row, 0, unroll=7)
        for group in range(0, per if left else 0, 4):
            count = min(4, per - group)
            at = per * main + group * left
            tile = block[at : at + count * left, :].astype(jnp.float32)
            for k in range(count):
                part = tile[k * left : (k + 1) * left, :]
                part = jnp.concatenate([part, jnp.zeros((16 - left, LANES), jnp.float32)], axis=0)
                fibres[
                    pl.ds(base + main, 16), (group + k) * LANES : (group + k + 1) * LANES
                ] = part.astype(jnp.bfloat16)

    at = 0
    for i in range(0, whole, STEP):
        product = lax.dot_general(
            fibres[i : i + STEP, :],
            fibres[i:, :],
            (((1,), (1,)), ((), ())),
            preferred_element_type=jnp.float32,
        )
        for j in range(0, whole - i, STEP):
            out[at : at + STEP, :] = out[at : at + STEP, :] + product[:, j : j + STEP]
            at += STEP


def gram(arrivals, carried, sources, pieces, share):
    pitch = len(pieces) * SUB
    whole = sources.shape[0] * pitch
    entries = [(i, places) for i, piece in enumerate(arrivals) for _, places in piece]
    inputs = [block for piece in arrivals for block, _ in piece]
    groups, size = inputs[0].shape[1:3]

    def body(sources, *rest):
        blocks, starts = [], []
        for ref, (i, places) in zip(rest, entries):
            for k, (dz, dy) in enumerate(places):
                blocks.append(ref.at[k, 0])
                starts.append(sources[2 * dz + dy] * pitch + i * SUB)
        if carried is None:
            out, fibres = rest[len(inputs) :]
            before = None
        else:
            before, out, fibres = rest[len(inputs) :]
        gram_kernel(pieces, share // groups, starts, blocks, before, out, fibres)

    specs = [
        pl.BlockSpec((len(places), 1, size, LANES), lambda g: (0, g, 0, 0)) for _, places in entries
    ]
    shape = (len(block_pairs(whole)) * STEP, STEP)
    square = pl.BlockSpec(shape, lambda g: (0, 0))
    extra = [] if carried is None else [carried]
    return pl.pallas_call(
        body,
        grid=(groups,),
        out_shape=jax.ShapeDtypeStruct(shape, jnp.float32),
        in_specs=[pl.BlockSpec(memory_space=pltpu.SMEM)]
        + specs
        + [square] * len(extra),
        out_specs=square,
        scratch_shapes=[pltpu.VMEM((whole, share // groups * LANES), jnp.bfloat16)],
        compiler_params=pltpu.CompilerParams(vmem_limit_bytes=VMEM_BYTES),
        cost_estimate=pl.CostEstimate(flops=0, bytes_accessed=0, transcendentals=0),
        name="gram",
    )(sources, *inputs, *extra)


def spread_row(block, row):
    return jnp.broadcast_to(block[row : row + 1, :], block.shape)


def spread_column(block, column):
    return jnp.broadcast_to(block[:, column : column + 1], block.shape)


def add_up(terms):
    while len(terms) > 1:
        pairs = [a + b for a, b in zip(terms[::2], terms[1::2])]
        terms = pairs + terms[len(pairs) * 2 :]
    return terms[0]


def factor_block(square, inverse):
    strips = len(square)
    height = square[0].shape[0]
    rows = lax.broadcasted_iota(jnp.int32, square[0].shape, 0)
    for t in range(strips):
        first = t * height
        a = square[t]
        columns = [spread_column(a, first + u) for u in range(height)]
        b = {(v, u): spread_row(columns[u], v) for u in range(height) for v in range(u + 1)}
        scale, r = [], {}
        for u in range(height):
            scale.append(lax.rsqrt(b[u, u]))
            for w in range(u + 1, height):
                r[u, w] = b[u, w] * scale[u]
            for v in range(u + 1, height):
                for w in range(v, height):
                    b[v, w] = b[v, w] - r[u, v] * r[u, w]
        inv = {}
        for v in range(height):
            for u in range(v):
                acc = r[u, v] * inv[u, u]
                for w in range(u + 1, v):
                    acc = acc + r[w, v] * inv[w, u]
                inv[v, u] = -(acc * scale[v])
            inv[v, v] = scale[v]
        ones, twos = [], []
        for u in range(height):
            weight = jnp.zeros_like(a)
            for v in range(u, height):
                weight = jnp.where(rows == v, inv[v, u], weight)
            ones.append(weight * spread_row(a, u))
            twos.append(weight * spread_row(inverse[t], u))
        new_square, new_inverse = add_up(ones), add_up(twos)
        square[t], inverse[t] = new_square, new_inverse
        rows_square = [spread_row(new_square, u) for u in range(height)]
        rows_inverse = [spread_row(new_inverse, u) for u in range(height)]
        for later in range(t + 1, strips):
            target = square[later]
            factors = []
            for u in range(height):
                x = spread_column(target, first + u)
                for w in range(u):
                    x = x - factors[w] * r[w, u]
                factors.append(x * scale[u])
            square[later] = target - add_up([f * row for f, row in zip(factors, rows_square)])
            inverse[later] = inverse[later] - add_up(
                [f * row for f, row in zip(factors, rows_inverse)]
            )


def exact_dot(left, right, contract):
    return lax.dot_general(
        left,
        right,
        (contract, ((), ())),
        precision=lax.Precision.HIGHEST,
        preferred_element_type=jnp.float32,
    )


def cholesky_kernel(slab, place, gram_sum, before, out, work):
    whole = work.shape[0]
    panels = whole // LANES
    at = 0
    for i, j in block_pairs(whole):
        work[i : i + STEP, j : j + STEP] = (
            before[i : i + STEP, j : j + STEP] + gram_sum[at : at + STEP, :]
        )
        at += STEP

    height = 8
    lane = lax.broadcasted_iota(jnp.int32, (height, LANES), 1)
    row = lax.broadcasted_iota(jnp.int32, (height, LANES), 0)
    columns = lax.broadcasted_iota(jnp.int32, (LANES, whole), 1)
    half = panels // 2 * LANES

    def one_panel(p, _):
        start = pl.multiple_of(p * LANES, LANES)
        strips = LANES // height
        square, inverse = [], []
        for t in range(strips):
            square.append(work[pl.ds(start + t * height, height), pl.ds(start, LANES)])
            inverse.append(jnp.where(lane == row + t * height, 1.0, 0.0))
        factor_block(square, inverse)
        inverse = jnp.concatenate(inverse, axis=0)
        done = exact_dot(inverse, work[pl.ds(start, LANES), :], ((1,), (0,)))
        done = jnp.where(columns >= start, done, 0.0)
        work[pl.ds(start, LANES), :] = done
        rest = jnp.where(columns >= start + LANES, done, 0.0)

        @pl.when(p + 1 < panels // 2)
        def _():
            work[:half, :] = work[:half, :] - exact_dot(rest[:, :half], done, ((0,), (0,)))

        @pl.when(p + 1 < panels)
        def _():
            work[half:, half:] = work[half:, half:] - exact_dot(
                rest[:, half:], done[:, half:], ((0,), (0,))
            )

        return 0

    lax.fori_loop(0, panels, one_panel, 0)
    first = pl.multiple_of(place[0] * slab, 8)
    rows = first + lax.broadcasted_iota(jnp.int32, (slab, whole), 0)
    columns = lax.broadcasted_iota(jnp.int32, (slab, whole), 1)
    out[...] = jnp.where(columns >= rows, work[pl.ds(first, slab), :], 0.0)


def cholesky_rows(gram_sum, before, place, slab):
    whole = before.shape[0]
    vmem = pl.BlockSpec(memory_space=pltpu.VMEM)
    return pl.pallas_call(
        functools.partial(cholesky_kernel, slab),
        out_shape=jax.ShapeDtypeStruct((slab, whole), jnp.float32),
        in_specs=[pl.BlockSpec(memory_space=pltpu.SMEM), vmem, vmem],
        out_specs=vmem,
        scratch_shapes=[pltpu.VMEM((whole, whole), jnp.float32)],
        compiler_params=pltpu.CompilerParams(vmem_limit_bytes=VMEM_BYTES),
        cost_estimate=pl.CostEstimate(flops=0, bytes_accessed=0, transcendentals=0),
        name="cholesky",
    )(place, gram_sum, before)


def slice_out(upper_r):
    row_block = upper_r.shape[0] // lax.axis_size("gy")
    col_block = upper_r.shape[1] // lax.axis_size("gx")
    return lax.dynamic_slice(
        upper_r,
        (lax.axis_index("gy") * row_block, lax.axis_index("gx") * col_block),
        (row_block, col_block),
    )


def finish(gram_sum, running_r):
    total = (
        jnp.dot(
            running_r.T,
            running_r,
            precision=lax.Precision.HIGHEST,
            preferred_element_type=jnp.float32,
        )
        + gram_sum
    )
    return slice_out(lax.linalg.cholesky(total.T, symmetrize_input=False).T)


def plain(fields, x_factor, running_r):
    exchanged = lax.all_to_all(fields, "gx", split_axis=2, concat_axis=0, tiled=True)
    full_x, middle, part_cells = exchanged.shape
    product = lax.dot_general(
        x_factor,
        exchanged.reshape(full_x, middle * part_cells),
        (((0,), (0,)), ((), ())),
        preferred_element_type=jnp.float32,
    )
    projected = product.astype(jnp.bfloat16).reshape(x_factor.shape[1], middle, part_cells)
    fibres = lax.all_to_all(projected, "gy", split_axis=2, concat_axis=1, tiled=True)
    local_gram = lax.dot_general(
        fibres, fibres, (((0, 2), (0, 2)), ((), ())), preferred_element_type=jnp.float32
    )
    return finish(lax.psum(local_gram, ("gx", "gy")), running_r)


def bit_of(axis, bit):
    return (lax.axis_index(axis) >> bit) & 1


def swap(value, axis, bit):
    flips = [(i, i ^ (1 << bit)) for i in range(lax.axis_size(axis))]
    return lax.ppermute(value, axis, flips)


def halve(value, axis, bit):
    halves = value.reshape(2, value.shape[0] // 2, value.shape[1])
    mine = bit_of(axis, bit)
    keep = lax.dynamic_index_in_dim(halves, mine, 0, keepdims=False)
    give = lax.dynamic_index_in_dim(halves, 1 - mine, 0, keepdims=False)
    return keep + swap(give, axis, bit)


def double(value, axis, bit):
    other = swap(value, axis, bit)
    return jnp.where(
        bit_of(axis, bit) == 0,
        jnp.concatenate([value, other]),
        jnp.concatenate([other, value]),
    )


def shift_slow(value, step, slow):
    n = slow * 2
    return lax.ppermute(value, "gy", [(i, (i + 2 * step) % n) for i in range(n)])


def sum_over_all(value):
    n_x, n_y = lax.axis_size("gx"), lax.axis_size("gy")
    bits = n_x.bit_length() - 1
    slow = n_y // 2
    mine = lax.axis_index("gy") // 2
    for bit in range(bits):
        value = halve(value, "gx", bit)
    value = halve(value, "gy", 0)
    rows, width = value.shape[0] // slow, value.shape[1]
    quarters = value.reshape(slow, rows, width)
    total = lax.dynamic_index_in_dim(quarters, mine, 0, keepdims=False)
    for step in range(1, slow):
        give = lax.dynamic_index_in_dim(quarters, (mine + step) % slow, 0, keepdims=False)
        total = total + shift_slow(give, step, slow)
    whole = jnp.zeros((slow, rows, width), value.dtype)
    whole = lax.dynamic_update_index_in_dim(whole, total, mine, 0)
    for step in range(1, slow):
        got = shift_slow(total, step, slow)
        whole = lax.dynamic_update_index_in_dim(whole, got, (mine + slow - step) % slow, 0)
    value = whole.reshape(slow * rows, width)
    value = double(value, "gy", 0)
    for bit in reversed(range(bits)):
        value = double(value, "gx", bit)
    return value


def pipelined(fields, x_factor, running_r):
    n_x, n_y = lax.axis_size("gx"), lax.axis_size("gy")
    me_x, me_y = lax.axis_index("gx"), lax.axis_index("gy")
    depth, rows, cells = fields.shape
    rank = x_factor.shape[1]
    share = rank // n_y
    cells_part = cells // n_x
    pieces = y_pieces(rows)
    by_y = jnp.transpose(fields, (1, 0, 2))

    factor = jnp.stack(
        [
            lax.dynamic_slice(x_factor, ((me_x ^ d) * depth, 0), (depth, rank)).T
            for d in range(n_x)
        ]
    )
    slow = n_y // 2
    shifts = [(dz, dy) for dz in range(slow) for dy in range(2)]

    def to(index, shift):
        return (index // 2 + shift[0]) % slow * 2 + (index % 2 + shift[1]) % 2

    def back(index, shift):
        return (index // 2 + slow - shift[0]) % slow * 2 + (index % 2 + shift[1]) % 2

    scalars = jnp.stack(
        [(me_x ^ d) * cells_part for d in range(n_x)] + [to(me_y, s) * share for s in shifts]
    ).astype(jnp.int32)
    sources = jnp.stack([back(me_y, s) for s in shifts]).astype(jnp.int32)

    chunks = [(cell, piece) for cell in range(0, cells_part, LANES) for piece in pieces]
    per_gram = len(pieces)

    size = pieces[0][1]
    full = running_r.shape[0]
    padding = ((0, 0), (0, 0), (0, SUB - size))
    wide_r = jnp.pad(running_r.reshape(full, -1, size), padding).reshape(full, -1)
    before = exact_dot(wide_r, wide_r, ((0,), (0,)))
    padded = jnp.arange(wide_r.shape[1]) % SUB >= size
    before = before + jnp.diag(padded.astype(jnp.float32))

    flown = []

    def start(operand, axis, pairs):
        slots = range(max(0, len(flown) - 2 * WINDOW + 1), max(0, len(flown) - WINDOW + 1))
        if slots:
            operand, *passed = lax.optimization_barrier((operand, *[flown[i] for i in slots]))
            flown[slots.start : slots.stop] = passed
        flown.append(lax.ppermute(operand, axis, pairs))
        return len(flown) - 1

    def start_x(partner, send):
        return start(send, "gx", [(i, i ^ partner) for i in range(n_x)])

    def start_y(shift, send):
        return start(send, "gy", [(i, to(i, shift)) for i in range(n_y)])

    moving = []
    for index, chunk in enumerate(chunks[:AHEAD]):
        sends = pack(by_y, scalars, chunk, n_x, [factor] if index else [])
        slots = []
        for (partner, _, _), send in zip(send_list(chunk, n_x), sends):
            slots.append(start_x(partner, send))
        moving.append(slots)
        if index == 0:
            near = [
                start_x(1, pack_near(by_y, scalars, cell)) for cell in range(0, cells_part, LANES)
            ]
    arrived = []
    carried = None

    def value_of(block):
        return flown[block] if isinstance(block, int) else block

    def cross(k, j):
        pair = [value_of(arrived[k][dz][0])[1] for dz in (2 * j, 2 * j + 1)]
        slot = start_y((0, 1), jnp.stack(pair))
        arrived[k].append((slot, ((2 * j, 1), (2 * j + 1, 1))))

    def add_gram(carried, first):
        group = arrived[first : first + per_gram]
        blocks = [[(value_of(block), places) for block, places in piece] for piece in group]
        return gram(blocks, carried, sources, pieces, share)

    for k, chunk in enumerate(chunks):
        following = chunks[k + AHEAD] if k + AHEAD < len(chunks) else None
        last = k == len(chunks) - 1
        after = [before] if k == 1 else []
        if k >= per_gram + 2 and (k - 2) % per_gram == 0:
            carried = add_gram(carried, k - 2 - per_gram)
            after.append(carried)
        outs, sends = project(
            by_y,
            flown[near[chunk[0] // LANES]],
            [flown[slot] for slot in moving[k]],
            factor,
            scalars,
            chunk,
            following,
            n_x,
            share,
            slow,
            last,
            after,
        )
        steps = []
        for i, place in enumerate(shifts if last else shifts[::2]):
            if i:
                steps.append((((i if last else [1, 3, 2][i - 1]) - (3.5 if k == 0 else 0.9)) / (len(outs) - 1), 0, i))
        for j in range(slow // 2 if k else 0):
            steps.append(((j + 0.5) / (slow // 2), 1, j))
        slots = [None] * len(sends)
        for i in range(len(sends)):
            steps.append(((i + 1.2) / len(sends), 2, i))
        landed = [(outs[0], ((0, 0),))] + [None] * (len(outs) - 1)
        arrived.append(landed)
        for _, kind, i in sorted(steps):
            if kind == 0:
                shift = shifts[i] if last else shifts[2 * i]
                landed[i] = (start_y(shift, outs[i]), (shift,))
            elif kind == 1:
                cross(k - 1, i)
            else:
                slots[i] = start_x(send_list(following, n_x)[i][0], sends[i])
        if sends:
            moving.append(slots)
    for first in range(0, len(chunks), per_gram):
        if first + per_gram + 2 >= len(chunks):
            carried = add_gram(carried, first)

    summed = sum_over_all(carried)
    slab = cholesky_rows(summed, before, me_y.astype(jnp.int32)[None], pitch_of(rows))
    groups = rows * n_y // n_x // size
    mine = lax.dynamic_slice(
        slab, (0, me_x * (groups * SUB)), (slab.shape[0], groups * SUB)
    )
    mine = mine.reshape(-1, SUB, groups, SUB)[:, :size, :, :size]
    return mine.reshape(rows, groups * size)


def on_device(fields, x_factor, running_r):
    n_x, n_y = lax.axis_size("gx"), lax.axis_size("gy")
    depth, rows, cells = fields.shape
    rank = x_factor.shape[1]
    fits = (
        cells % (n_x * LANES) == 0
        and rank % (2 * n_y) == 0
        and depth % 8 == 0
        and n_x & (n_x - 1) == 0
        and n_x >= 4
        and n_y % 4 == 0
        and rows >= 16
        and rows % (4 * len(y_pieces(rows))) == 0
        and n_y * pitch_of(rows) % STEP == 0
        and rows * n_y // n_x % y_pieces(rows)[0][1] == 0
        and len(block_pairs(n_y * pitch_of(rows))) * STEP % (8 * n_x * n_y) == 0
    )
    if fits:
        return pipelined(fields, x_factor, running_r)
    return plain(fields, x_factor, running_r)


def solution(mesh):
    in_specs = (P("gx", "gy", None), P(), P())
    out_specs = P("gy", "gx")
    return jax.shard_map(
        on_device, mesh=mesh, in_specs=in_specs, out_specs=out_specs, check_vma=False
    )
```

```python
import functools

import jax
import jax.numpy as jnp
from jax import lax
from jax.experimental import pallas as pl
from jax.experimental.pallas import tpu as pltpu
from jax.sharding import PartitionSpec as P

LANES = 128
SUB = 32
STEP = 256
WINDOW = 5
AHEAD = 2
VMEM_BYTES = 56 * 1024 * 1024


def y_pieces(rows):
    count = -(-rows // SUB)
    size = rows // count
    return [(i * size, size) for i in range(count)]


def pitch_of(rows):
    return len(y_pieces(rows)) * SUB


def send_list(chunk, n_x):
    rows = chunk[1][1]
    half = rows // 2
    return [(partner, at, half) for at in (0, half) for partner in range(2, n_x)]


def copy_cells(fields, out, scalars, partner, cell, start, size, sem):
    column = pl.multiple_of(scalars[partner] + cell, LANES)
    return pltpu.make_async_copy(
        fields.at[pl.ds(start, size), :, pl.ds(column, LANES)], out, sem
    )


def chunk_copies(fields, outs, scalars, chunk, n_x, sems):
    cell, (start, _) = chunk
    return [
        copy_cells(fields, outs[i], scalars, partner, cell, start + at, size, sems.at[i])
        for i, (partner, at, size) in enumerate(send_list(chunk, n_x))
    ]


def run_pack(fields, scalars, shapes, make_copies, after=()):
    def body(scalars, fields, *rest):
        rest = rest[len(after) :]
        copies = make_copies(fields, rest[:-1], scalars, rest[-1])
        for copy in copies:
            copy.start()
        for copy in copies:
            copy.wait()

    return pl.pallas_call(
        body,
        out_shape=shapes,
        in_specs=[pl.BlockSpec(memory_space=pltpu.SMEM)]
        + [pl.BlockSpec(memory_space=pl.ANY)] * (1 + len(after)),
        out_specs=[pl.BlockSpec(memory_space=pltpu.VMEM)] * len(shapes),
        scratch_shapes=[pltpu.SemaphoreType.DMA((len(shapes),))],
        compiler_params=pltpu.CompilerParams(vmem_limit_bytes=VMEM_BYTES),
        cost_estimate=pl.CostEstimate(flops=0, bytes_accessed=0, transcendentals=0),
        name="pack",
    )(scalars, fields, *after)


def send_shapes(chunk, n_x, depth):
    return [
        jax.ShapeDtypeStruct((size, depth, LANES), jnp.bfloat16)
        for _, _, size in send_list(chunk, n_x)
    ]


def pack(fields, scalars, chunk, n_x, after):
    return run_pack(
        fields,
        scalars,
        send_shapes(chunk, n_x, fields.shape[1]),
        lambda fields, outs, scalars, sems: chunk_copies(fields, outs, scalars, chunk, n_x, sems),
        after,
    )


def pack_near(fields, scalars, cell):
    rows, depth = fields.shape[:2]
    return run_pack(
        fields,
        scalars,
        [jax.ShapeDtypeStruct((rows, depth, LANES), jnp.bfloat16)],
        lambda fields, outs, scalars, sems: [
            copy_cells(fields, outs[0], scalars, 1, cell, 0, rows, sems.at[0])
        ],
    )[0]


def project_kernel(chunk, following, n_x, rank, share, scalars, fields, near, got, factor, outs, sends, own, other, wide, held, sems, out_sems):
    cell, (start, rows) = chunk
    copies = [
        copy_cells(fields, own, scalars, 0, cell, start, rows, sems.at[0]),
        pltpu.make_async_copy(near.at[pl.ds(start, rows)], other, sems.at[1]),
    ]
    for copy in copies:
        copy.start()
    packing = []
    if following is not None:
        packing = chunk_copies(
            fields, held, scalars, following, n_x, sems.at[pl.ds(2, len(sends))]
        )
    for copy in packing:
        copy.start()
    for copy in copies:
        copy.wait()

    leaving = []
    half = rows // 2
    many = max(n for n in range(1, 9) if half % n == 0)
    for start_row in (0, half):
        blocks = [(0, own, 0), (1, other, 0)]
        for (partner, at, _), block in zip(send_list(chunk, n_x), got):
            if at == start_row:
                blocks.append((partner, block, at))

        def one_group(group, _):
            y = start_row + group * many
            total = None
            for partner, block, at in blocks:
                right = jnp.concatenate([block[y - at + k] for k in range(many)], axis=1)
                term = jnp.dot(factor[partner], right, preferred_element_type=jnp.float32)
                total = term if total is None else total + term
            for k in range(many):
                at = pl.multiple_of((y + k) * rank, 8)
                wide[pl.ds(at, rank), :] = total[:, k * LANES : (k + 1) * LANES]
            return 0

        lax.fori_loop(0, half // many, one_group, 0)
        if start_row == 0:
            for i, copy in enumerate(packing):
                copy.wait()
                leaving.append(pltpu.make_async_copy(held[i], sends[i], out_sems.at[i]))
                leaving[i].start()

    main = rows // 16 * 16
    left = rows - main
    halves = [out.at[i] for out in outs for i in range(out.shape[0])]
    groups = halves[0].shape[0]
    per = share // groups
    for part, at_group in [(p, g) for p in range(len(halves)) for g in range(groups)]:
        out = halves[part].at[at_group]
        first = scalars[n_x + part] + at_group * per

        def one_row(i, _):
            picked = wide[pl.ds(first + i, main, stride=rank), :]
            out[pl.ds(pl.multiple_of(i * main, 16), main), :] = picked.astype(jnp.bfloat16)
            return 0

        lax.fori_loop(0, per, one_row, 0, unroll=7)
        for four in range(0, per if left else 0, 4):
            count = min(4, per - four)
            tile = [
                wide[pl.ds(main * rank + first + four + k, left, stride=rank), :]
                for k in range(count)
            ]
            tile = jnp.concatenate(tile, axis=0).astype(jnp.bfloat16)
            at = per * main + four * left
            out[at : at + count * left, :] = tile
    for copy in leaving:
        copy.wait()


def project(fields, near, got, factor, scalars, chunk, following, n_x, share, slow, apart):
    rows = chunk[1][1]
    rank = factor.shape[1]
    depth = fields.shape[1]
    n_got = len(got)
    n_sends = 0 if following is None else n_got
    n_outs = 2 * slow if apart else slow
    vmem = pl.BlockSpec(memory_space=pltpu.VMEM)
    any_space = pl.BlockSpec(memory_space=pl.ANY)

    def body(scalars, fields, near, *rest):
        got = rest[:n_got]
        factor = rest[n_got]
        rest = rest[n_got + 1 :]
        outs = rest[:n_outs]
        sends = rest[n_outs : n_outs + n_sends]
        own, other, wide, sems, out_sems = rest[n_outs + n_sends : n_outs + n_sends + 5]
        held = rest[n_outs + n_sends + 5 :]
        project_kernel(
            chunk, following, n_x, rank, share, scalars, fields, near, got, factor, outs, sends, own, other, wide, held, sems, out_sems
        )

    groups = column_groups(share)
    shape = (1 if apart else 2, groups, share // groups * rows, LANES)
    shapes = [jax.ShapeDtypeStruct(shape, jnp.bfloat16)] * n_outs
    if following is not None:
        shapes += send_shapes(following, n_x, depth)
    outs = pl.pallas_call(
        body,
        out_shape=shapes,
        in_specs=[pl.BlockSpec(memory_space=pltpu.SMEM), any_space, any_space]
        + [vmem] * (n_got + 1),
        out_specs=[vmem] * n_outs + [any_space] * n_sends,
        scratch_shapes=[
            pltpu.VMEM((rows, depth, LANES), jnp.bfloat16),
            pltpu.VMEM((rows, depth, LANES), jnp.bfloat16),
            pltpu.VMEM((-(-rows // 8) * 8 * rank, LANES), jnp.float32),
            pltpu.SemaphoreType.DMA((2 + n_got,)),
            pltpu.SemaphoreType.DMA((n_got,)),
        ]
        + [pltpu.VMEM(shape.shape, shape.dtype) for shape in shapes[n_outs:]],
        compiler_params=pltpu.CompilerParams(vmem_limit_bytes=VMEM_BYTES),
        cost_estimate=pl.CostEstimate(flops=0, bytes_accessed=0, transcendentals=0),
        name="project",
    )(scalars, fields, near, *got, factor)
    return outs[:n_outs], outs[n_outs:]


def column_groups(share):
    return 3 if share % 6 == 0 else 1


def block_pairs(whole):
    return [(i, j) for i in range(0, whole, STEP) for j in range(i, whole, STEP)]


def gram_kernel(pieces, per, places, blocks, carried, out, fibres):
    whole = fibres.shape[0]
    rows = pieces[0][1]
    main = rows // 16 * 16
    left = rows - main

    @pl.when(pl.program_id(0) == 0)
    def _():
        out[...] = jnp.zeros_like(out) if carried is None else carried[...]

    for place, block in zip(places, blocks):
        base = pl.multiple_of(place, 16)

        def one_row(i, _):
            at = pl.multiple_of(i * LANES, LANES)
            fibres[pl.ds(base, main), pl.ds(at, LANES)] = block[
                pl.ds(pl.multiple_of(i * main, 16), main), :
            ]
            return 0

        lax.fori_loop(0, per, one_row, 0, unroll=7)
        for group in range(0, per if left else 0, 4):
            count = min(4, per - group)
            at = per * main + group * left
            tile = block[at : at + count * left, :].astype(jnp.float32)
            for k in range(count):
                part = tile[k * left : (k + 1) * left, :]
                part = jnp.concatenate([part, jnp.zeros((16 - left, LANES), jnp.float32)], axis=0)
                fibres[
                    pl.ds(base + main, 16), (group + k) * LANES : (group + k + 1) * LANES
                ] = part.astype(jnp.bfloat16)

    at = 0
    for i in range(0, whole, STEP):
        product = lax.dot_general(
            fibres[i : i + STEP, :],
            fibres[i:, :],
            (((1,), (1,)), ((), ())),
            preferred_element_type=jnp.float32,
        )
        for j in range(0, whole - i, STEP):
            out[at : at + STEP, :] = out[at : at + STEP, :] + product[:, j : j + STEP]
            at += STEP


def gram(arrivals, carried, sources, pieces, share):
    pitch = len(pieces) * SUB
    whole = sources.shape[0] * pitch
    entries = [(i, places) for i, piece in enumerate(arrivals) for _, places in piece]
    inputs = [block for piece in arrivals for block, _ in piece]
    groups, size = inputs[0].shape[1:3]

    def body(sources, *rest):
        blocks, starts = [], []
        for ref, (i, places) in zip(rest, entries):
            for k, (dz, dy) in enumerate(places):
                blocks.append(ref.at[k, 0])
                starts.append(sources[2 * dz + dy] * pitch + i * SUB)
        if carried is None:
            out, fibres = rest[len(inputs) :]
            before = None
        else:
            before, out, fibres = rest[len(inputs) :]
        gram_kernel(pieces, share // groups, starts, blocks, before, out, fibres)

    specs = [
        pl.BlockSpec((len(places), 1, size, LANES), lambda g: (0, g, 0, 0)) for _, places in entries
    ]
    shape = (len(block_pairs(whole)) * STEP, STEP)
    square = pl.BlockSpec(shape, lambda g: (0, 0))
    extra = [] if carried is None else [carried]
    return pl.pallas_call(
        body,
        grid=(groups,),
        out_shape=jax.ShapeDtypeStruct(shape, jnp.float32),
        in_specs=[pl.BlockSpec(memory_space=pltpu.SMEM)]
        + specs
        + [square] * len(extra),
        out_specs=square,
        scratch_shapes=[pltpu.VMEM((whole, share // groups * LANES), jnp.bfloat16)],
        compiler_params=pltpu.CompilerParams(vmem_limit_bytes=VMEM_BYTES),
        cost_estimate=pl.CostEstimate(flops=0, bytes_accessed=0, transcendentals=0),
        name="gram",
    )(sources, *inputs, *extra)


def spread_row(block, row):
    return jnp.broadcast_to(block[row : row + 1, :], block.shape)


def spread_column(block, column):
    return jnp.broadcast_to(block[:, column : column + 1], block.shape)


def add_up(terms):
    while len(terms) > 1:
        pairs = [a + b for a, b in zip(terms[::2], terms[1::2])]
        terms = pairs + terms[len(pairs) * 2 :]
    return terms[0]


def factor_block(square, inverse):
    strips = len(square)
    height = square[0].shape[0]
    rows = lax.broadcasted_iota(jnp.int32, square[0].shape, 0)
    for t in range(strips):
        first = t * height
        a = square[t]
        columns = [spread_column(a, first + u) for u in range(height)]
        b = {(v, u): spread_row(columns[u], v) for u in range(height) for v in range(u + 1)}
        scale, r = [], {}
        for u in range(height):
            scale.append(lax.rsqrt(b[u, u]))
            for w in range(u + 1, height):
                r[u, w] = b[u, w] * scale[u]
            for v in range(u + 1, height):
                for w in range(v, height):
                    b[v, w] = b[v, w] - r[u, v] * r[u, w]
        inv = {}
        for v in range(height):
            for u in range(v):
                acc = r[u, v] * inv[u, u]
                for w in range(u + 1, v):
                    acc = acc + r[w, v] * inv[w, u]
                inv[v, u] = -(acc * scale[v])
            inv[v, v] = scale[v]
        ones, twos = [], []
        for u in range(height):
            weight = jnp.zeros_like(a)
            for v in range(u, height):
                weight = jnp.where(rows == v, inv[v, u], weight)
            ones.append(weight * spread_row(a, u))
            twos.append(weight * spread_row(inverse[t], u))
        new_square, new_inverse = add_up(ones), add_up(twos)
        square[t], inverse[t] = new_square, new_inverse
        rows_square = [spread_row(new_square, u) for u in range(height)]
        rows_inverse = [spread_row(new_inverse, u) for u in range(height)]
        for later in range(t + 1, strips):
            target = square[later]
            factors = []
            for u in range(height):
                x = spread_column(target, first + u)
                for w in range(u):
                    x = x - factors[w] * r[w, u]
                factors.append(x * scale[u])
            square[later] = target - add_up([f * row for f, row in zip(factors, rows_square)])
            inverse[later] = inverse[later] - add_up(
                [f * row for f, row in zip(factors, rows_inverse)]
            )


def exact_dot(left, right, contract):
    return lax.dot_general(
        left,
        right,
        (contract, ((), ())),
        precision=lax.Precision.HIGHEST,
        preferred_element_type=jnp.float32,
    )


def cholesky_kernel(slab, place, gram_sum, before, out, work):
    whole = work.shape[0]
    panels = whole // LANES
    at = 0
    for i, j in block_pairs(whole):
        work[i : i + STEP, j : j + STEP] = (
            before[i : i + STEP, j : j + STEP] + gram_sum[at : at + STEP, :]
        )
        at += STEP

    height = 8
    lane = lax.broadcasted_iota(jnp.int32, (height, LANES), 1)
    row = lax.broadcasted_iota(jnp.int32, (height, LANES), 0)
    columns = lax.broadcasted_iota(jnp.int32, (LANES, whole), 1)
    half = panels // 2 * LANES

    def one_panel(p, _):
        start = pl.multiple_of(p * LANES, LANES)
        strips = LANES // height
        square, inverse = [], []
        for t in range(strips):
            square.append(work[pl.ds(start + t * height, height), pl.ds(start, LANES)])
            inverse.append(jnp.where(lane == row + t * height, 1.0, 0.0))
        factor_block(square, inverse)
        inverse = jnp.concatenate(inverse, axis=0)
        done = exact_dot(inverse, work[pl.ds(start, LANES), :], ((1,), (0,)))
        done = jnp.where(columns >= start, done, 0.0)
        work[pl.ds(start, LANES), :] = done
        rest = jnp.where(columns >= start + LANES, done, 0.0)

        @pl.when(p + 1 < panels // 2)
        def _():
            work[:half, :] = work[:half, :] - exact_dot(rest[:, :half], done, ((0,), (0,)))

        @pl.when(p + 1 < panels)
        def _():
            work[half:, half:] = work[half:, half:] - exact_dot(
                rest[:, half:], done[:, half:], ((0,), (0,))
            )

        return 0

    lax.fori_loop(0, panels, one_panel, 0)
    first = pl.multiple_of(place[0] * slab, 8)
    rows = first + lax.broadcasted_iota(jnp.int32, (slab, whole), 0)
    columns = lax.broadcasted_iota(jnp.int32, (slab, whole), 1)
    out[...] = jnp.where(columns >= rows, work[pl.ds(first, slab), :], 0.0)


def cholesky_rows(gram_sum, before, place, slab):
    whole = before.shape[0]
    vmem = pl.BlockSpec(memory_space=pltpu.VMEM)
    return pl.pallas_call(
        functools.partial(cholesky_kernel, slab),
        out_shape=jax.ShapeDtypeStruct((slab, whole), jnp.float32),
        in_specs=[pl.BlockSpec(memory_space=pltpu.SMEM), vmem, vmem],
        out_specs=vmem,
        scratch_shapes=[pltpu.VMEM((whole, whole), jnp.float32)],
        compiler_params=pltpu.CompilerParams(vmem_limit_bytes=VMEM_BYTES),
        cost_estimate=pl.CostEstimate(flops=0, bytes_accessed=0, transcendentals=0),
        name="cholesky",
    )(place, gram_sum, before)


def slice_out(upper_r):
    row_block = upper_r.shape[0] // lax.axis_size("gy")
    col_block = upper_r.shape[1] // lax.axis_size("gx")
    return lax.dynamic_slice(
        upper_r,
        (lax.axis_index("gy") * row_block, lax.axis_index("gx") * col_block),
        (row_block, col_block),
    )


def finish(gram_sum, running_r):
    total = (
        jnp.dot(
            running_r.T,
            running_r,
            precision=lax.Precision.HIGHEST,
            preferred_element_type=jnp.float32,
        )
        + gram_sum
    )
    return slice_out(lax.linalg.cholesky(total.T, symmetrize_input=False).T)


def plain(fields, x_factor, running_r):
    exchanged = lax.all_to_all(fields, "gx", split_axis=2, concat_axis=0, tiled=True)
    full_x, middle, part_cells = exchanged.shape
    product = lax.dot_general(
        x_factor,
        exchanged.reshape(full_x, middle * part_cells),
        (((0,), (0,)), ((), ())),
        preferred_element_type=jnp.float32,
    )
    projected = product.astype(jnp.bfloat16).reshape(x_factor.shape[1], middle, part_cells)
    fibres = lax.all_to_all(projected, "gy", split_axis=2, concat_axis=1, tiled=True)
    local_gram = lax.dot_general(
        fibres, fibres, (((0, 2), (0, 2)), ((), ())), preferred_element_type=jnp.float32
    )
    return finish(lax.psum(local_gram, ("gx", "gy")), running_r)


def bit_of(axis, bit):
    return (lax.axis_index(axis) >> bit) & 1


def swap(value, axis, bit):
    flips = [(i, i ^ (1 << bit)) for i in range(lax.axis_size(axis))]
    return lax.ppermute(value, axis, flips)


def halve(value, axis, bit):
    halves = value.reshape(2, value.shape[0] // 2, value.shape[1])
    mine = bit_of(axis, bit)
    keep = lax.dynamic_index_in_dim(halves, mine, 0, keepdims=False)
    give = lax.dynamic_index_in_dim(halves, 1 - mine, 0, keepdims=False)
    return keep + swap(give, axis, bit)


def double(value, axis, bit):
    other = swap(value, axis, bit)
    return jnp.where(
        bit_of(axis, bit) == 0,
        jnp.concatenate([value, other]),
        jnp.concatenate([other, value]),
    )


def shift_slow(value, step, slow):
    n = slow * 2
    return lax.ppermute(value, "gy", [(i, (i + 2 * step) % n) for i in range(n)])


def sum_over_all(value):
    n_x, n_y = lax.axis_size("gx"), lax.axis_size("gy")
    bits = n_x.bit_length() - 1
    slow = n_y // 2
    mine = lax.axis_index("gy") // 2
    for bit in range(bits):
        value = halve(value, "gx", bit)
    value = halve(value, "gy", 0)
    rows, width = value.shape[0] // slow, value.shape[1]
    quarters = value.reshape(slow, rows, width)
    total = lax.dynamic_index_in_dim(quarters, mine, 0, keepdims=False)
    for step in range(1, slow):
        give = lax.dynamic_index_in_dim(quarters, (mine + step) % slow, 0, keepdims=False)
        total = total + shift_slow(give, step, slow)
    whole = jnp.zeros((slow, rows, width), value.dtype)
    whole = lax.dynamic_update_index_in_dim(whole, total, mine, 0)
    for step in range(1, slow):
        got = shift_slow(total, step, slow)
        whole = lax.dynamic_update_index_in_dim(whole, got, (mine + slow - step) % slow, 0)
    value = whole.reshape(slow * rows, width)
    value = double(value, "gy", 0)
    for bit in reversed(range(bits)):
        value = double(value, "gx", bit)
    return value


def pipelined(fields, x_factor, running_r):
    n_x, n_y = lax.axis_size("gx"), lax.axis_size("gy")
    me_x, me_y = lax.axis_index("gx"), lax.axis_index("gy")
    depth, rows, cells = fields.shape
    rank = x_factor.shape[1]
    share = rank // n_y
    cells_part = cells // n_x
    pieces = y_pieces(rows)
    by_y = jnp.transpose(fields, (1, 0, 2))

    factor = jnp.stack(
        [
            lax.dynamic_slice(x_factor, ((me_x ^ d) * depth, 0), (depth, rank)).T
            for d in range(n_x)
        ]
    )
    slow = n_y // 2
    shifts = [(dz, dy) for dz in range(slow) for dy in range(2)]

    def to(index, shift):
        return (index // 2 + shift[0]) % slow * 2 + (index % 2 + shift[1]) % 2

    def back(index, shift):
        return (index // 2 + slow - shift[0]) % slow * 2 + (index % 2 + shift[1]) % 2

    scalars = jnp.stack(
        [(me_x ^ d) * cells_part for d in range(n_x)] + [to(me_y, s) * share for s in shifts]
    ).astype(jnp.int32)
    sources = jnp.stack([back(me_y, s) for s in shifts]).astype(jnp.int32)

    chunks = [(cell, piece) for cell in range(0, cells_part, LANES) for piece in pieces]
    per_gram = len(pieces)

    size = pieces[0][1]
    full = running_r.shape[0]
    padding = ((0, 0), (0, 0), (0, SUB - size))
    wide_r = jnp.pad(running_r.reshape(full, -1, size), padding).reshape(full, -1)
    before = exact_dot(wide_r, wide_r, ((0,), (0,)))
    padded = jnp.arange(wide_r.shape[1]) % SUB >= size
    before = before + jnp.diag(padded.astype(jnp.float32))

    flown = []

    def start(operand, axis, pairs):
        slots = range(max(0, len(flown) - 2 * WINDOW + 1), max(0, len(flown) - WINDOW + 1))
        if slots:
            operand, *passed = lax.optimization_barrier((operand, *[flown[i] for i in slots]))
            flown[slots.start : slots.stop] = passed
        flown.append(lax.ppermute(operand, axis, pairs))
        return len(flown) - 1

    def start_x(partner, send):
        return start(send, "gx", [(i, i ^ partner) for i in range(n_x)])

    def start_y(shift, send):
        return start(send, "gy", [(i, to(i, shift)) for i in range(n_y)])

    moving = []
    for index, chunk in enumerate(chunks[:AHEAD]):
        sends = pack(by_y, scalars, chunk, n_x, [factor, before] if index else [])
        slots = []
        for (partner, _, _), send in zip(send_list(chunk, n_x), sends):
            slots.append(start_x(partner, send))
        moving.append(slots)
        if index == 0:
            near = [
                start_x(1, pack_near(by_y, scalars, cell)) for cell in range(0, cells_part, LANES)
            ]
    arrived = []
    carried = None

    def value_of(block):
        return flown[block] if isinstance(block, int) else block

    def cross(k, j, with_gram=None):
        pair = [value_of(arrived[k][dz][0])[1] for dz in (2 * j, 2 * j + 1)]
        send = jnp.stack(pair)
        if with_gram is not None:
            send, with_gram = lax.optimization_barrier((send, with_gram))
        slot = start_y((0, 1), send)
        arrived[k].append((slot, ((2 * j, 1), (2 * j + 1, 1))))
        return with_gram

    def add_gram(carried, first):
        group = arrived[first : first + per_gram]
        blocks = [[(value_of(block), places) for block, places in piece] for piece in group]
        return gram(blocks, carried, sources, pieces, share)

    for k, chunk in enumerate(chunks):
        following = chunks[k + AHEAD] if k + AHEAD < len(chunks) else None
        last = k == len(chunks) - 1
        outs, sends = project(
            by_y,
            flown[near[chunk[0] // LANES]],
            [flown[slot] for slot in moving[k]],
            factor,
            scalars,
            chunk,
            following,
            n_x,
            share,
            slow,
            last,
        )
        steps = []
        for i, place in enumerate(shifts if last else shifts[::2]):
            if i:
                steps.append((((i if last else [1, 3, 2][i - 1]) - (3.5 if k == 0 else 0.9)) / (len(outs) - 1), 0, i))
        for j in range(slow // 2 if k else 0):
            steps.append(((j + 0.5) / (slow // 2), 1, j))
        slots = [None] * len(sends)
        for i in range(len(sends)):
            steps.append(((i + 1.2) / len(sends), 2, i))
        landed = [(outs[0], ((0, 0),))] + [None] * (len(outs) - 1)
        arrived.append(landed)
        for _, kind, i in sorted(steps):
            if kind == 0:
                shift = shifts[i] if last else shifts[2 * i]
                landed[i] = (start_y(shift, outs[i]), (shift,))
            elif kind == 1:
                if i == slow // 2 - 1 and k > per_gram and k % per_gram == 1:
                    carried = add_gram(carried, k - 1 - per_gram)
                    carried = cross(k - 1, i, carried)
                else:
                    cross(k - 1, i)
            else:
                slots[i] = start_x(send_list(following, n_x)[i][0], sends[i])
        if sends:
            moving.append(slots)
    for first in range(0, len(chunks), per_gram):
        if first + per_gram + 1 >= len(chunks):
            carried = add_gram(carried, first)

    summed = sum_over_all(carried)
    slab = cholesky_rows(summed, before, me_y.astype(jnp.int32)[None], pitch_of(rows))
    groups = rows * n_y // n_x // size
    mine = lax.dynamic_slice(
        slab, (0, me_x * (groups * SUB)), (slab.shape[0], groups * SUB)
    )
    mine = mine.reshape(-1, SUB, groups, SUB)[:, :size, :, :size]
    return mine.reshape(rows, groups * size)


def on_device(fields, x_factor, running_r):
    n_x, n_y = lax.axis_size("gx"), lax.axis_size("gy")
    depth, rows, cells = fields.shape
    rank = x_factor.shape[1]
    fits = (
        cells % (n_x * LANES) == 0
        and rank % (2 * n_y) == 0
        and depth % 8 == 0
        and n_x & (n_x - 1) == 0
        and n_x >= 4
        and n_y % 4 == 0
        and rows >= 16
        and rows % (4 * len(y_pieces(rows))) == 0
        and n_y * pitch_of(rows) % STEP == 0
        and rows * n_y // n_x % y_pieces(rows)[0][1] == 0
        and len(block_pairs(n_y * pitch_of(rows))) * STEP % (8 * n_x * n_y) == 0
    )
    if fits:
        return pipelined(fields, x_factor, running_r)
    return plain(fields, x_factor, running_r)


def solution(mesh):
    in_specs = (P("gx", "gy", None), P(), P())
    out_specs = P("gy", "gx")
    return jax.shard_map(
        on_device, mesh=mesh, in_specs=in_specs, out_specs=out_specs, check_vma=False
    )
```
